512 devices in a mesh: grp: 16 (over x, z_hi, core), slab: 32 (over y, z_lo).
Axes of the slice: x: 4, y: 4, z: 16 (z_hi: 2, z_lo: 8; z = z_hi * 8 + z_lo), core: 2. Of those that a mesh axis runs over, the one named last changes fastest.
Arguments:
- orbitals: bfloat16 [512, 32768], P(('grp', 'slab')), may hold values from -6 to 6
- offsets: int32 [512, 3], replicated, may hold values from 0 to 8
- slot_pairs: int32 [3072, 2], P(('grp', 'slab')), may hold values from -1 to 511, as said below
Outputs:
- exchange_field: float32 [512, 32768], P(('grp', 'slab'))
- gram: float32 [16, 32, 32], P('grp', None, 'slab')
The draws below stay inside these ranges and needn't reach their ends.
Inputs may be any that keep to these rules, and one draw needn't show every extreme that they name: `slot_pairs`: rows 6 * d to 6 * d + 5 are the slots of device d (grp index times 32 plus slab index). A slot holds two orbital ids i != j, or -1 in both columns when empty. i lies in the slot's group (id // 32); j in the same group or in the next one (group indices wrap). Each group has exactly 160 filled slots, and some device of each group has all 6 slots filled.
All inputs are finite; a program needn't handle non-finite values.
Results may differ from the reference program's by a relative error of at most 0.0003.
Values may be sent and summed in bfloat16 or wider, within the bound.
A program may use at most 64 MiB of HBM per device.

```python
import functools
import math
import jax
import jax.numpy as jnp
from jax import lax

SIDE = 32
SHIFT = 8
CHEB = 6
SLOTS = 6
CELLS = 32768
GROUPS = 16
ORB_GRP = 32
NORB = 512
LIVE = 160
PAIR_SLOTS = 3072


def draw_slot_pairs(key, part):
    slot_total = ORB_GRP * SLOTS

    def one_group(group_index):
        group_key = jax.random.fold_in(jax.random.fold_in(key, 17), group_index)
        keys = jax.random.split(group_key, 6)
        full_member = jax.random.randint(keys[0], (), 0, ORB_GRP)
        slot_ids = jnp.arange(slot_total, dtype=jnp.int32)
        in_full = slot_ids // SLOTS == full_member
        scores = jax.random.permutation(keys[1], slot_total).astype(jnp.int32)
        scores = jnp.where(in_full, scores + slot_total, scores)
        order_index = jnp.argsort(scores, stable=True)
        ranking = jnp.zeros((slot_total,), jnp.int32).at[order_index].set(slot_ids)
        live_slot = in_full | (ranking < LIVE - SLOTS)
        left_local = jax.random.randint(keys[2], (slot_total,), 0, ORB_GRP)
        step_size = jax.random.randint(keys[3], (slot_total,), 1, ORB_GRP)
        crossing = jax.random.randint(keys[4], (slot_total,), 0, 2)
        other_local = jax.random.randint(keys[5], (slot_total,), 0, ORB_GRP)
        right_group = jnp.where(crossing == 1, (group_index + 1) % GROUPS, group_index)
        right_local = jnp.where(crossing == 1, other_local, (left_local + step_size) % ORB_GRP)
        paired = jnp.stack((group_index * ORB_GRP + left_local, right_group * ORB_GRP + right_local), 1)
        return jnp.where(live_slot[:, None], paired, -1).astype(jnp.int32)
    groups_all = jax.vmap(one_group)(jnp.arange(GROUPS, dtype=jnp.int32))
    return groups_all.reshape(PAIR_SLOTS, 2)


def plant(entries, rng, least, high):
    place = [jax.random.randint(jax.random.fold_in(rng, axis), (), 0, length) for axis, length in enumerate(entries.shape)]
    widest = entries.shape.index(max(entries.shape))
    next_to = place[:widest] + [(place[widest] + 1) % entries.shape[widest]] + place[widest + 1:]
    return entries.at[tuple(place)].set(least).at[tuple(next_to)].set(high)


def block_levels(key, dims, cuts, least, top_value):
    def one(dim, blocks):
        draws = jax.random.uniform(jax.random.fold_in(jax.random.fold_in(key, 6), dim), (blocks,), jnp.float32, least / len(cuts), top_value / len(cuts))
        return jnp.repeat(jnp.exp(draws), dims[dim] // blocks).reshape((-1,) + (1,) * (len(dims) - dim - 1))

    loudness = one(*cuts[0])
    for cut in cuts[1:]:
        loudness = loudness * one(*cut)
    return loudness


def gaussian(stream_key, shape, deviation, most, cuts=(), kind=jnp.bfloat16):
    drawn = deviation * jax.random.normal(stream_key, shape, jnp.float32)
    if cuts:
        drawn = drawn * block_levels(stream_key, shape, cuts, -0.22, 0.18)
    return jnp.clip(drawn, -most, most).astype(kind)


def setup_inputs(seed: int = 0) -> dict:
    arg_keys = jax.random.split(jax.random.key(seed), 4)
    return {
        "orbitals": gaussian(arg_keys[0], (NORB, CELLS), 1.0, 6.0, ((0, 512),)),
        "offsets": plant(jax.random.randint(arg_keys[1], (NORB, 3), 0, SHIFT + 1), jax.random.fold_in(arg_keys[1], 1), 0, SHIFT).astype(jnp.int32),
        "slot_pairs": draw_slot_pairs(jax.random.fold_in(arg_keys[3], 71), 0),
    }


stencil_terms = ((1, 1.5), (2, -0.15), (3, 1.0 / 90.0))
center_term = -49.0 / 18.0

def slide_cells(values, offset, dim_index):
    extent = values.shape[dim_index]
    pad_shape = list(values.shape)
    pad_shape[dim_index] = abs(offset)
    zero_part = jnp.zeros(pad_shape, values.dtype)
    if offset > 0:
        kept_part = lax.slice_in_dim(values, offset, extent, axis=dim_index)
        return jnp.concatenate((kept_part, zero_part), dim_index)
    kept_part = lax.slice_in_dim(values, 0, extent + offset, axis=dim_index)
    return jnp.concatenate((zero_part, kept_part), dim_index)

def operator(values, box_edge):
    outer_dim = values.ndim - 2
    inner_dim = values.ndim - 1
    zcoord = lax.broadcasted_iota(jnp.int32, (box_edge * box_edge,), 0) % box_edge
    stencil_sum = 3.0 * center_term * values
    for offset, weight in stencil_terms:
        beside = slide_cells(values, offset, outer_dim) + slide_cells(values, -offset, outer_dim)
        beside = beside + slide_cells(values, offset * box_edge, inner_dim) + slide_cells(values, -offset * box_edge, inner_dim)
        upper_part = jnp.where(zcoord + offset < box_edge, slide_cells(values, offset, inner_dim), 0.0)
        lower_part = jnp.where(zcoord - offset >= 0, slide_cells(values, -offset, inner_dim), 0.0)
        stencil_sum = stencil_sum + weight * (beside + upper_part + lower_part)
    return -stencil_sum

def coefficients(box_edge, sweeps):
    lowest = 3.0 * (math.pi / (box_edge + 1)) ** 2
    highest = 18.2
    center_value = 0.5 * (highest + lowest)
    half_width = 0.5 * (highest - lowest)
    alpha_list = [1.0 / center_value]
    beta_list = [0.0]
    for step_index in range(1, sweeps):
        previous = alpha_list[-1]
        if step_index == 1:
            beta_now = 0.5 * (half_width * previous) ** 2
        else:
            beta_now = (0.5 * half_width * previous) ** 2
        alpha_list.append(1.0 / (center_value - beta_now / previous))
        beta_list.append(beta_now)
    return (alpha_list, beta_list)

def chebyshev_solve(density, box_edge, sweeps):
    alpha_list, beta_list = coefficients(box_edge, sweeps)
    alpha_table = jnp.asarray(alpha_list, jnp.float32)
    beta_table = jnp.asarray(beta_list, jnp.float32)

    def advance(step_index, state):
        solution, residual, search = state
        search = residual + beta_table[step_index] * search
        solution = solution + alpha_table[step_index] * search
        residual = residual - alpha_table[step_index] * operator(search, box_edge)
        return (solution, residual, search)
    start = (jnp.zeros_like(density), density, jnp.zeros_like(density))
    return lax.fori_loop(0, sweeps, advance, start)[0]

def place_box(box, offset_gap, box_edge, margin):
    cube = box.reshape(box_edge, box_edge, box_edge)
    padded = jnp.pad(cube, margin)
    start = (margin - offset_gap).astype(jnp.int32)
    moved = lax.dynamic_slice(padded, (start[0], start[1], start[2]), (box_edge, box_edge, box_edge))
    return moved.reshape(box_edge, box_edge * box_edge)

def reference(orbitals, offsets, slot_pairs):
    box_edge = SIDE
    shaped = functools.partial(place_box, box_edge=box_edge, margin=SHIFT)
    live_slot = slot_pairs[:, 0] >= 0
    order_index = jnp.argsort(jnp.where(live_slot, 0, 1).astype(jnp.int32), stable=True)[:GROUPS * LIVE]
    chosen_pairs = slot_pairs[order_index]

    def add_pair(fields, slot_pair):
        left_id = slot_pair[0]
        right_id = slot_pair[1]
        offset_gap = offsets[right_id] - offsets[left_id]
        left_box = orbitals[left_id].reshape(box_edge, box_edge * box_edge).astype(jnp.float32)
        right_box = shaped(orbitals[right_id], offset_gap).astype(jnp.float32)
        potential = chebyshev_solve(left_box * right_box, box_edge, CHEB)
        fields = fields.at[left_id].add((potential * right_box).reshape(CELLS))
        fields = fields.at[right_id].add(shaped(potential * left_box, -offset_gap).reshape(CELLS))
        return (fields, None)
    exchange_field, _ = lax.scan(add_pair, jnp.zeros((NORB, CELLS), jnp.float32), chosen_pairs)
    group_first = jnp.arange(NORB, dtype=jnp.int32) // ORB_GRP * ORB_GRP
    shifts = offsets - offsets[group_first]
    framed_orbital = jax.vmap(shaped)(orbitals, shifts).reshape(GROUPS, ORB_GRP, CELLS)
    framed_field = jax.vmap(shaped)(exchange_field, shifts).astype(jnp.bfloat16).reshape(GROUPS, ORB_GRP, CELLS)
    gram = jnp.einsum('gac,gbc->gab', framed_orbital.astype(jnp.float32), framed_field.astype(jnp.float32), precision=lax.Precision.HIGHEST)
    return (exchange_field, gram / math.sqrt(CELLS))
```

```python
import math

import jax
import jax.numpy as jnp
import numpy as np
from jax import lax
from jax.experimental import pallas as pl
from jax.experimental.pallas import tpu as pltpu
from jax.sharding import PartitionSpec as P

SIDE = 32
PLANE = SIDE * SIDE
CELLS = SIDE * PLANE
CHEB = 6
GROUPS = 16
ORB = 32
PAIRS = 160
PART = 40
BLOCK = 32
F32, BF16, I32 = jnp.float32, jnp.bfloat16, jnp.int32
MESH = pl.DeviceIdType.MESH

NN = (((1,), (0,)), ((), ()))
NT = (((1,), (1,)), ((), ()))
TN = (((0,), (0,)), ((), ()))


def operator_1d():
    weights = {0: -49.0 / 18.0, 1: 1.5, 2: -0.15, 3: 1.0 / 90.0}
    a = np.zeros((SIDE, SIDE))
    for i in range(SIDE):
        for j in range(SIDE):
            a[i, j] = -weights.get(abs(i - j), 0.0)
    return a


def eigen(a):
    a, n = a.copy(), a.shape[0]
    v = np.eye(n)
    for _ in range(10):
        for p in range(n - 1):
            for q in range(p + 1, n):
                if abs(a[p, q]) < 1e-18:
                    continue
                theta = (a[q, q] - a[p, p]) / (2.0 * a[p, q])
                t = (1.0 if theta >= 0 else -1.0) / (abs(theta) + math.sqrt(theta * theta + 1.0))
                c = 1.0 / math.sqrt(t * t + 1.0)
                s = t * c
                ap, aq = a[:, p].copy(), a[:, q].copy()
                a[:, p], a[:, q] = c * ap - s * aq, s * ap + c * aq
                ap, aq = a[p].copy(), a[q].copy()
                a[p], a[q] = c * ap - s * aq, s * ap + c * aq
                vp, vq = v[:, p].copy(), v[:, q].copy()
                v[:, p], v[:, q] = c * vp - s * vq, s * vp + c * vq
    return np.diag(a).copy(), v


def polynomial(lam):
    low, high = 3.0 * (math.pi / (SIDE + 1)) ** 2, 18.2
    mid, half = 0.5 * (high + low), 0.5 * (high - low)
    alpha, beta = 1.0 / mid, 0.0
    x, res, p = np.zeros_like(lam), np.ones_like(lam), np.zeros_like(lam)
    for k in range(1, CHEB + 1):
        if k > 1:
            beta = 0.5 * (half * alpha) ** 2 if k == 2 else (0.5 * half * alpha) ** 2
            alpha = 1.0 / (mid - beta / alpha)
        p = res + beta * p
        x = x + alpha * p
        res = res - alpha * lam * p
    return x


def halves(a):
    high = a.astype(BF16)
    low = (a - high.astype(np.float64)).astype(BF16)
    return np.stack([high, low])


def constants():
    lam, q = eigen(operator_1d())
    plane = halves(np.kron(q, q))
    lines = halves(np.stack([np.kron(q.T, np.eye(8)), np.kron(q, np.eye(8))]))
    total = lam[:, None, None] + lam[None, :, None] + lam[None, None, :]
    table = polynomial(total).reshape(SIDE, PLANE).astype(np.float32)
    return plane, lines, table


def iota(shape, dim):
    return lax.broadcasted_iota(I32, shape, dim)


def roll(x, n, axis):
    n %= x.shape[axis]
    return pltpu.roll(x, n, axis) if n else x


def lead(x, n):
    n %= x.shape[0]
    return jnp.concatenate([x[x.shape[0] - n :], x[: x.shape[0] - n]], 0) if n else x


def bit(o, b):
    return jnp.bitwise_and(jnp.right_shift(o, b), 1) > 0


def turn_rows(x, o2, o3, sign):
    third = jnp.bitwise_and(iota(x.shape, 1), SIDE - 1)
    b2 = jnp.broadcast_to(o2, x.shape)
    b3 = jnp.broadcast_to(o3, x.shape)
    for b in range(4):
        n = 1 << b
        x = jnp.where(bit(b2, b), roll(x, sign * SIDE * n, 1), x)
        inside = third >= n if sign > 0 else third < SIDE - n
        y = jnp.where(inside, roll(x, sign * n, 1), roll(x, sign * (n - SIDE), 1))
        x = jnp.where(bit(b3, b), y, x)
    return x


def turn_box(x, o, sign):
    o1, o2, o3 = (jnp.broadcast_to(v, x.shape) for v in o)
    lane = iota(x.shape, 2)
    third = jnp.bitwise_and(lane, SIDE - 1)
    for b in range(4):
        n = 1 << b
        x = jnp.where(bit(o1, b), lead(x, sign * n), x)
        if b < 2:
            y = roll(x, sign * SIDE * n, 2)
            kept = lane >= SIDE * n if sign > 0 else lane < 128 - SIDE * n
            y = jnp.where(kept, y, roll(y, sign, 1))
        else:
            y = roll(x, sign * n // 4, 1)
        x = jnp.where(bit(o2, b), y, x)
        inside = third >= n if sign > 0 else third < SIDE - n
        y = jnp.where(inside, roll(x, sign * n, 2), roll(x, sign * (n - SIDE), 2))
        x = jnp.where(bit(o3, b), y, x)
    return x


def turn_lead(x, o1, sign):
    o = jnp.broadcast_to(o1, x.shape[1:])[None]
    for b in range(4):
        x = jnp.where(bit(o, b), lead(x, sign << b if sign > 0 else -(1 << b)), x)
    return x


def split(x):
    high = x.astype(BF16)
    return high, (x - high.astype(F32)).astype(BF16)


def dot(a, b, dims=NN):
    return lax.dot_general(a, b, dims, preferred_element_type=F32)


def device(x, y, z, c):
    return x * 4 + lax.div(z, 8) * 2 + c, y * 8 + lax.rem(z, 8)


def kernel(
    box_ref, offsets_ref, slots_ref, plane_ref, lines_ref, table_ref,
    field_ref, gram_ref,
    plane, lines, own, mid, near_out, far_out, near_in, far_in, cells,
    ohl, ohr, offs, lm, rm, dh, dl, modes, lines_in, lines_out, back,
    field, far_field, prev_field, tiles, gp, send6, mid6, send7, fin,
    const_sem, send1, recv1, send2, recv2, send3, recv3, send4, recv4, send5, recv5, send6s, recv6, send7s, recv7,
):
    gi, si = lax.axis_index("grp"), lax.axis_index("slab")
    x, zh, core = lax.div(gi, 4), lax.rem(lax.div(gi, 2), 2), lax.rem(gi, 2)
    y, zl = lax.div(si, 8), lax.rem(si, 8)
    z = zh * 8 + zl
    q = x * 4 + y
    rho = q * 2 + core
    role = z
    nxt = lax.rem(role + 1, GROUPS)

    const1 = pltpu.make_async_copy(plane_ref, plane, const_sem.at[0])
    const2 = pltpu.make_async_copy(lines_ref, lines, const_sem.at[1])
    const1.start()
    const2.start()

    row = iota((72, 512), 0)
    local = lax.rem(row, ORB)
    ident = jnp.where(row < ORB, role, nxt) * ORB + lax.rem(local, 4) * 8 + lax.div(local, 4)
    ident = jnp.where(row < 2 * ORB, ident, gi * ORB + si)
    pick = (ident == iota((72, 512), 1)).astype(BF16)
    found = dot(pick, offsets_ref[...].astype(BF16))
    own_o = [found[64:65, d : d + 1].astype(I32).reshape(1, 1, 1) for d in range(3)]

    box = turn_box(box_ref[...].astype(F32).reshape(SIDE, 8, 128), own_o, 1)
    own[:, 0] = box.reshape(16, 16, 128).astype(BF16)
    slots = slots_ref[...]
    member = lax.rem(slots, ORB)
    spot = lax.rem(member, 8) * 4 + lax.div(member, 8)
    spot = spot + jnp.where(lax.div(slots, ORB) == gi, 0, ORB)
    spot = jnp.where(slots >= 0, spot, -1).astype(F32)
    own[:, 1] = jnp.broadcast_to(jnp.concatenate([spot, spot], 0).astype(BF16)[None], (16, 16, 128))

    pltpu.make_async_copy(own.at[q], mid.at[q], recv1).start()
    for t in range(1, 16):
        peer = lax.rem(q + t, 16)
        pltpu.make_async_remote_copy(
            own.at[peer], mid.at[q], send1, recv1, device(lax.div(peer, 4), lax.rem(peer, 4), z, core), MESH
        ).start()
    pltpu.make_async_copy(mid, mid, recv1).wait()

    heap = mid[:, 0].astype(F32).reshape(4, 4, 2, 8, 128)
    lists = mid[:, 1].astype(F32)[:, :8].reshape(4, 4, 8, 128)
    lane8 = iota((8, 128), 1)
    for g in range(4):
        merged = lists[g, 0]
        for j in range(1, 4):
            merged = jnp.where(lax.div(lane8, 2) == j, roll(lists[g, j], 2 * j, 1), merged)
        merged = jnp.concatenate([merged, merged], 0).astype(BF16)
        for c in range(2):
            part = heap[g, :, c].reshape(2, 16, 128).astype(BF16)
            near_out[g, c, 0:2] = part
            near_out[g, c, 2] = merged
            far_out[g, c] = part
    sends2 = []
    for g in range(4):
        for c in range(2):
            for far in range(2):
                target = lax.rem(g * 4 + zh * 2 + core + GROUPS - far, GROUPS)
                here = jnp.logical_and(target == z, core == c)
                out = (near_out, far_out)[far].at[g, c]
                into = (near_in, far_in)[far].at[zl]
                remote = pltpu.make_async_remote_copy(
                    out, into, send2.at[g, c, far], recv2.at[far], device(x, y, target, c), MESH
                )
                local_copy = pltpu.make_async_copy(out, into, recv2.at[far])
                pl.when(here)(local_copy.start)
                pl.when(jnp.logical_not(here))(remote.start)
                sends2.append((here, remote))
    pltpu.make_async_copy(own.at[pl.ds(0, 15)], own.at[pl.ds(0, 15)], send1).wait()
    pltpu.make_async_copy(near_in, near_in, recv2.at[0]).wait()
    pltpu.make_async_copy(far_in, far_in, recv2.at[1]).wait()

    lists = near_in[:, 2].astype(F32)[:, :8].reshape(64, 128)
    left = jnp.concatenate([lists[:, 2 * j : 2 * j + 1] for j in range(4)], 0)
    right = jnp.concatenate([lists[:, 2 * j + 1 : 2 * j + 2] for j in range(4)], 0)
    row = iota((64, 1), 0)
    used = lax.rem(row, 8) < 6
    used = jnp.concatenate([used.astype(F32)] * 4, 0)
    live = jnp.logical_and(left >= 0, used > 0)
    live_f = jnp.where(live, 1.0, 0.0)
    before = (iota((256, 256), 1) < iota((256, 256), 0)).astype(BF16)
    rank = dot(before, jnp.broadcast_to(live_f, (256, 128)).astype(BF16))[:, 0:1]
    rank = jnp.where(live, rank, -1.0)
    chosen = (jnp.broadcast_to(rank, (256, 256)) == iota((256, 256), 1).astype(F32)).astype(BF16)
    orbital = iota((256, 128), 1).astype(F32)
    pick_l = (jnp.broadcast_to(left, (256, 128)) == orbital).astype(BF16)
    pick_r = (jnp.broadcast_to(right, (256, 128)) == orbital).astype(BF16)
    one_l = dot(chosen, pick_l, TN)[:PAIRS]
    one_r = dot(chosen, pick_r, TN)[:PAIRS]
    ohl[...] = one_l
    ohr[...] = one_r
    o3 = jnp.concatenate([found[:64], jnp.zeros((64, found.shape[1]), F32)], 0)
    offs[...] = jnp.broadcast_to(dot(one_l.astype(BF16), o3.astype(BF16))[:, :3], (PAIRS, 3)).astype(I32)

    cells[0:256] = near_in[:, 0:2].astype(F32).reshape(256, 128)
    cells[256:512] = far_in[...].astype(F32).reshape(256, 128)
    orbs = jnp.concatenate([cells[pl.ds(r, 64, stride=8), :] for r in range(8)], 1)
    lane = iota((64, PLANE), 1)
    o = [jnp.broadcast_to(found[:64, d : d + 1], (64, PLANE)) for d in range(3)]
    code = jnp.where(rho.astype(F32) < o[0], 1.0, 0.0)
    code = code + jnp.where(lax.div(lane, SIDE).astype(F32) < o[1], 2.0, 0.0)
    code = code + jnp.where(jnp.bitwise_and(lane, SIDE - 1).astype(F32) < o[2], 4.0, 0.0)
    both = jnp.concatenate([orbs, code], 1).astype(BF16)
    both = jnp.concatenate([both, jnp.zeros((64, 2 * PLANE), BF16)], 0)

    for b in range(PAIRS // BLOCK):
        rows = slice(b * BLOCK, (b + 1) * BLOCK)
        lv = dot(ohl[rows].astype(BF16), both)
        rv = dot(ohr[rows].astype(BF16), both)
        same = lv[:, PLANE:] == rv[:, PLANE:]
        lmv = jnp.where(same, lv[:, :PLANE], 0.0)
        rmv = jnp.where(same, rv[:, :PLANE], 0.0)
        lm[rows] = lmv
        rm[rows] = rmv
        dens = turn_rows(lmv * rmv, offs[rows, 1:2], offs[rows, 2:3], -1)
        dh[rows], dl[rows] = split(dens)

    const1.wait()
    const2.wait()
    for n in range(4):
        cols = slice(n * 256, (n + 1) * 256)
        wh, wl = plane[0, :, cols], plane[1, :, cols]
        modes[:, cols] = dot(dh[...], wh) + dot(dl[...], wh) + dot(dh[...], wl)

    def part_of(ref, r):
        return ref.at[pl.ds(pl.multiple_of(lax.div(r, 8) * PART, 8), PART), pl.ds(pl.multiple_of(lax.rem(r, 8) * 128, 128), 128)]

    def device_of(r):
        return device(lax.div(r, 8), lax.rem(lax.div(r, 2), 4), z, lax.rem(r, 2))

    pltpu.make_async_copy(part_of(modes, rho), lines_in.at[rho], recv3).start()

    @pl.loop(1, 32)
    def _(t):
        r = lax.rem(rho + t, 32)
        pltpu.make_async_remote_copy(part_of(modes, r), lines_in.at[rho], send3, recv3, device_of(r), MESH).start()

    pltpu.make_async_copy(lines_in, lines_in, recv3).wait()

    u, v = lax.div(rho, 8), lax.rem(rho, 8)
    scale = table_ref[:, pl.ds(pl.multiple_of(v * 128, 128), 128)]
    scale = jnp.broadcast_to(scale[:, None, :], (SIDE, 8, 128)).reshape(256, 128)
    for j in range(PART // 8):
        rows = slice(8 * j, 8 * j + 8)
        o1 = offs[pl.ds(pl.multiple_of(u * PART, 8) + 8 * j, 8), 0:1]
        s = turn_lead(lines_in[:, rows, :], o1, -1).reshape(256, 128)
        for way in range(2):
            sh, sl = split(s)
            s = dot(lines[0, way], sh) + dot(lines[0, way], sl) + dot(lines[1, way], sh)
            if way == 0:
                s = s * scale
        lines_out[:, rows, :] = turn_lead(s.reshape(SIDE, 8, 128), o1, 1)

    pltpu.make_async_copy(lines_out.at[rho], part_of(back, rho), recv4).start()

    @pl.loop(1, 32)
    def _(t):
        r = lax.rem(rho + t, 32)
        pltpu.make_async_remote_copy(lines_out.at[r], part_of(back, rho), send4, recv4, device_of(r), MESH).start()

    pltpu.make_async_copy(lines_in.at[pl.ds(0, 31)], lines_in.at[pl.ds(0, 31)], send3).wait()
    pltpu.make_async_copy(back, back, recv4).wait()

    bh, bl = split(back[...])
    dh[...] = bh
    dl[...] = bl
    for n in range(4):
        cols = slice(n * 256, (n + 1) * 256)
        wh, wl = plane[0, cols, :], plane[1, cols, :]
        modes[:, cols] = dot(dh[...], wh, NT) + dot(dl[...], wh, NT) + dot(dh[...], wl, NT)

    total = None
    for b in range(PAIRS // BLOCK):
        rows = slice(b * BLOCK, (b + 1) * BLOCK)
        pot = turn_rows(modes[rows], offs[rows, 1:2], offs[rows, 2:3], 1)
        term = None
        for one, other in ((ohl, rm), (ohr, lm)):
            ch, cl = split(pot * other[rows])
            pick = one[rows].astype(BF16)
            new = dot(pick, ch, TN) + dot(pick, cl, TN)
            term = new if term is None else term + new
        total = term if total is None else total + term
    field[...] = total[0:ORB]
    far_field[...] = total[ORB : 2 * ORB]

    far_copy = pltpu.make_async_remote_copy(far_field, prev_field, send5, recv5, device(x, y, nxt, core), MESH)
    far_copy.start()
    framed = jnp.where(code[:ORB] == code[0:1], orbs[:ORB], 0.0)
    perm_row = iota((128, ORB), 0)
    perm = (lax.rem(perm_row, 8) * 4 + lax.div(perm_row, 8) == iota((128, ORB), 1)) & (perm_row < ORB)
    framed = dot(perm.astype(BF16), framed.astype(BF16)).astype(BF16)
    far_copy.wait_recv()
    summed = field[...] + prev_field[...]
    framed_field = jnp.where(code[:ORB] == code[0:1], summed, 0.0).astype(BF16)
    gp[0:ORB] = dot(framed_field, framed, NT)
    gp[ORB : ORB + 8] = jnp.zeros((8, 128), F32)
    for r in range(8):
        tiles[pl.ds(r, ORB, stride=8), :] = summed[:, r * 128 : (r + 1) * 128]

    home_x, home_zh, home_c = lax.div(role, 4), lax.rem(lax.div(role, 2), 2), lax.rem(role, 2)
    sends6 = []
    for k in range(8):
        send6[k, 0:4] = tiles[32 * k : 32 * k + 32].reshape(4, 8, 128)
        send6[k, 4] = gp[4 * k : 4 * k + 8]
        target = home_zh * 8 + k
        here = jnp.logical_and(target == z, home_c == core)
        into = mid6.at[home_x * 2 + core]
        remote = pltpu.make_async_remote_copy(
            send6.at[k], into, send6s.at[k], recv6, device(x, y, target, home_c), MESH
        )
        local_copy = pltpu.make_async_copy(send6.at[k], into, recv6)
        pl.when(here)(local_copy.start)
        pl.when(jnp.logical_not(here))(remote.start)
        sends6.append((here, remote))
    pltpu.make_async_copy(mid6, mid6, recv6).wait()
    for g in range(4):
        gram_tile = mid6[2 * g, 4] + mid6[2 * g + 1, 4]
        for j in range(4):
            send7[4 * g + j, 0] = mid6[2 * g, j]
            send7[4 * g + j, 1] = mid6[2 * g + 1, j]
            send7[4 * g + j, 2] = gram_tile
    pltpu.make_async_copy(send7.at[q], fin.at[q], recv7).start()
    for t in range(1, 16):
        peer = lax.rem(q + t, 16)
        pltpu.make_async_remote_copy(
            send7.at[peer], fin.at[q], send7s, recv7, device(lax.div(peer, 4), lax.rem(peer, 4), z, core), MESH
        ).start()
    pltpu.make_async_copy(fin, fin, recv7).wait()
    result = turn_box(fin[:, 0:2].reshape(SIDE, 8, 128), own_o, -1)
    field_ref[...] = result.reshape(256, 128)
    gram_tile = fin[0, 2]
    for k in range(1, 16):
        gram_tile = gram_tile + fin[k, 2]
    gram_tile = jnp.where(iota((8, 128), 0) == y, gram_tile, 0.0)
    gram_ref[...] = jnp.sum(gram_tile, axis=0, keepdims=True) * (1.0 / math.sqrt(CELLS))

    for here, remote in sends2 + sends6:
        pl.when(jnp.logical_not(here))(remote.wait_send)
    pltpu.make_async_copy(lines_in.at[pl.ds(0, 31)], lines_in.at[pl.ds(0, 31)], send4).wait()
    far_copy.wait_send()
    pltpu.make_async_copy(fin.at[pl.ds(0, 15)], fin.at[pl.ds(0, 15)], send7s).wait()


def on_device(orbitals, offsets, slot_pairs):
    plane_c, lines_c, table_c = constants()
    slots = jnp.pad(slot_pairs, ((0, 2), (0, 126)), constant_values=-1)
    vmem = pl.BlockSpec(memory_space=pltpu.VMEM)
    hbm = pl.BlockSpec(memory_space=pl.ANY)
    dma = pltpu.SemaphoreType.DMA
    scratch = [
        pltpu.VMEM((2, PLANE, PLANE), BF16),
        pltpu.VMEM((2, 2, 256, 256), BF16),
        pltpu.VMEM((16, 2, 16, 128), BF16),
        pltpu.VMEM((16, 2, 16, 128), BF16),
        pltpu.VMEM((4, 2, 3, 16, 128), BF16),
        pltpu.VMEM((4, 2, 2, 16, 128), BF16),
        pltpu.VMEM((8, 3, 16, 128), BF16),
        pltpu.VMEM((8, 2, 16, 128), BF16),
        pltpu.VMEM((512, 128), F32),
        pltpu.VMEM((PAIRS, 128), F32),
        pltpu.VMEM((PAIRS, 128), F32),
        pltpu.VMEM((PAIRS, 3), I32),
        pltpu.VMEM((PAIRS, PLANE), F32),
        pltpu.VMEM((PAIRS, PLANE), F32),
        pltpu.VMEM((PAIRS, PLANE), BF16),
        pltpu.VMEM((PAIRS, PLANE), BF16),
        pltpu.VMEM((PAIRS, PLANE), F32),
        pltpu.VMEM((32, PART, 128), F32),
        pltpu.VMEM((32, PART, 128), F32),
        pltpu.VMEM((PAIRS, PLANE), F32),
        pltpu.VMEM((ORB, PLANE), F32),
        pltpu.VMEM((ORB, PLANE), F32),
        pltpu.VMEM((ORB, PLANE), F32),
        pltpu.VMEM((256, 128), F32),
        pltpu.VMEM((ORB + 8, 128), F32),
        pltpu.VMEM((8, 5, 8, 128), F32),
        pltpu.VMEM((8, 5, 8, 128), F32),
        pltpu.VMEM((16, 3, 8, 128), F32),
        pltpu.VMEM((16, 3, 8, 128), F32),
        dma((2,)),
        dma, dma,
        dma((4, 2, 2)), dma((2,)),
        dma, dma,
        dma, dma,
        dma, dma,
        dma((8,)), dma,
        dma, dma,
    ]
    field, gram = pl.pallas_call(
        kernel,
        out_shape=(jax.ShapeDtypeStruct((256, 128), F32), jax.ShapeDtypeStruct((1, 128), F32)),
        in_specs=[vmem, vmem, vmem, hbm, hbm, vmem],
        out_specs=(vmem, vmem),
        scratch_shapes=scratch,
        compiler_params=pltpu.CompilerParams(has_side_effects=True, vmem_limit_bytes=48 * 2**20),
    )(
        orbitals.reshape(256, 128),
        offsets,
        slots,
        jnp.asarray(plane_c),
        jnp.asarray(lines_c),
        jnp.asarray(table_c),
    )
    return field.reshape(1, CELLS), gram[0, :ORB].reshape(1, ORB, 1)


def solution(mesh):
    return jax.shard_map(
        on_device,
        mesh=mesh,
        in_specs=(P(("grp", "slab"), None), P(), P(("grp", "slab"), None)),
        out_specs=(P(("grp", "slab"), None), P("grp", None, "slab")),
        check_vma=False,
    )
```

```python
import math

import jax
import jax.numpy as jnp
import numpy as np
from jax import lax
from jax.experimental import pallas as pl
from jax.experimental.pallas import tpu as pltpu
from jax.sharding import PartitionSpec as P

SIDE = 32
PLANE = SIDE * SIDE
CELLS = SIDE * PLANE
CHEB = 6
GROUPS = 16
ORB = 32
PAIRS = 160
PART = 40
BLOCK = 32
F32, BF16, I32 = jnp.float32, jnp.bfloat16, jnp.int32
MESH = pl.DeviceIdType.MESH

NN = (((1,), (0,)), ((), ()))
NT = (((1,), (1,)), ((), ()))
TN = (((0,), (0,)), ((), ()))


def operator_1d():
    weights = {0: -49.0 / 18.0, 1: 1.5, 2: -0.15, 3: 1.0 / 90.0}
    a = np.zeros((SIDE, SIDE))
    for i in range(SIDE):
        for j in range(SIDE):
            a[i, j] = -weights.get(abs(i - j), 0.0)
    return a


def eigen(a):
    a, n = a.copy(), a.shape[0]
    v = np.eye(n)
    for _ in range(10):
        for p in range(n - 1):
            for q in range(p + 1, n):
                if abs(a[p, q]) < 1e-18:
                    continue
                theta = (a[q, q] - a[p, p]) / (2.0 * a[p, q])
                t = (1.0 if theta >= 0 else -1.0) / (abs(theta) + math.sqrt(theta * theta + 1.0))
                c = 1.0 / math.sqrt(t * t + 1.0)
                s = t * c
                ap, aq = a[:, p].copy(), a[:, q].copy()
                a[:, p], a[:, q] = c * ap - s * aq, s * ap + c * aq
                ap, aq = a[p].copy(), a[q].copy()
                a[p], a[q] = c * ap - s * aq, s * ap + c * aq
                vp, vq = v[:, p].copy(), v[:, q].copy()
                v[:, p], v[:, q] = c * vp - s * vq, s * vp + c * vq
    return np.diag(a).copy(), v


def polynomial(lam):
    low, high = 3.0 * (math.pi / (SIDE + 1)) ** 2, 18.2
    mid, half = 0.5 * (high + low), 0.5 * (high - low)
    alpha, beta = 1.0 / mid, 0.0
    x, res, p = np.zeros_like(lam), np.ones_like(lam), np.zeros_like(lam)
    for k in range(1, CHEB + 1):
        if k > 1:
            beta = 0.5 * (half * alpha) ** 2 if k == 2 else (0.5 * half * alpha) ** 2
            alpha = 1.0 / (mid - beta / alpha)
        p = res + beta * p
        x = x + alpha * p
        res = res - alpha * lam * p
    return x


def halves(a):
    high = a.astype(BF16)
    low = (a - high.astype(np.float64)).astype(BF16)
    return np.stack([high, low])


def constants():
    lam, q = eigen(operator_1d())
    plane = halves(np.kron(q, q))
    lines = halves(np.stack([np.kron(q.T, np.eye(8)), np.kron(q, np.eye(8))]))
    total = lam[:, None, None] + lam[None, :, None] + lam[None, None, :]
    table = polynomial(total).reshape(SIDE, PLANE).astype(np.float32)
    return plane, lines, table


def iota(shape, dim):
    return lax.broadcasted_iota(I32, shape, dim)


def roll(x, n, axis):
    n %= x.shape[axis]
    return pltpu.roll(x, n, axis) if n else x


def lead(x, n):
    n %= x.shape[0]
    return jnp.concatenate([x[x.shape[0] - n :], x[: x.shape[0] - n]], 0) if n else x


def bit(o, b):
    return jnp.bitwise_and(jnp.right_shift(o, b), 1) > 0


def turn_rows(x, o2, o3, sign):
    third = jnp.bitwise_and(iota(x.shape, 1), SIDE - 1)
    b2 = jnp.broadcast_to(o2, x.shape)
    b3 = jnp.broadcast_to(o3, x.shape)
    for b in range(4):
        n = 1 << b
        x = jnp.where(bit(b2, b), roll(x, sign * SIDE * n, 1), x)
        inside = third >= n if sign > 0 else third < SIDE - n
        y = jnp.where(inside, roll(x, sign * n, 1), roll(x, sign * (n - SIDE), 1))
        x = jnp.where(bit(b3, b), y, x)
    return x


def turn_box(x, o, sign):
    o1, o2, o3 = (jnp.broadcast_to(v, x.shape) for v in o)
    lane = iota(x.shape, 2)
    third = jnp.bitwise_and(lane, SIDE - 1)
    for b in range(4):
        n = 1 << b
        x = jnp.where(bit(o1, b), lead(x, sign * n), x)
        if b < 2:
            y = roll(x, sign * SIDE * n, 2)
            kept = lane >= SIDE * n if sign > 0 else lane < 128 - SIDE * n
            y = jnp.where(kept, y, roll(y, sign, 1))
        else:
            y = roll(x, sign * n // 4, 1)
        x = jnp.where(bit(o2, b), y, x)
        inside = third >= n if sign > 0 else third < SIDE - n
        y = jnp.where(inside, roll(x, sign * n, 2), roll(x, sign * (n - SIDE), 2))
        x = jnp.where(bit(o3, b), y, x)
    return x


def turn_lead(x, o1, sign):
    o = jnp.broadcast_to(o1, x.shape[1:])[None]
    for b in range(4):
        x = jnp.where(bit(o, b), lead(x, sign << b if sign > 0 else -(1 << b)), x)
    return x


def split(x):
    high = x.astype(BF16)
    return high, (x - high.astype(F32)).astype(BF16)


def dot(a, b, dims=NN):
    return lax.dot_general(a, b, dims, preferred_element_type=F32)


def rotated(x, y, core, t):
    m = lax.rem(t * 5, 16)
    return (
        lax.rem(x + lax.div(m, 4), 4),
        lax.rem(y + lax.rem(m, 4), 4),
        lax.rem(core + lax.div(t, 16), 2),
    )


def device(x, y, z, c):
    return x * 4 + lax.div(z, 8) * 2 + c, y * 8 + lax.rem(z, 8)


def kernel(
    box_ref, offsets_ref, slots_ref, plane_ref, lines_ref, table_ref,
    field_ref, gram_ref,
    plane, lines, table, own, mid, pair_out, boxes_out, pair_in, near_in, far_in, cells,
    ohl, ohr, offs, lm, rm, dh, dl, eh, el, modes, lines_in, lines_out, back,
    far_field, prev_field, tiles, gp, send6, mid6, fin, gram_out, gram_mid, gram_fwd, gram_fin,
    const_sem, send1, recv1, send2, recv2, send3, recv3, send4, recv4, send5, recv5,
    send6s, recv6, send6g, recv6g, send7s, recv7, send7g, recv7g,
):
    gi, si = lax.axis_index("grp"), lax.axis_index("slab")
    x, zh, core = lax.div(gi, 4), lax.rem(lax.div(gi, 2), 2), lax.rem(gi, 2)
    y, zl = lax.div(si, 8), lax.rem(si, 8)
    z = zh * 8 + zl
    q = x * 4 + y
    rho = q * 2 + core
    role = z
    nxt = lax.rem(role + 1, GROUPS)

    entry = pltpu.get_barrier_semaphore()

    @pl.loop(1, 32)
    def _(t):
        peer = rotated(x, y, core, t)
        pl.semaphore_signal(entry, 1, device_id=device(peer[0], peer[1], z, peer[2]), device_id_type=MESH)

    @pl.loop(1, 16)
    def _(t):
        for c in range(2):
            pl.semaphore_signal(entry, 1, device_id=device(x, y, lax.rem(z + t, 16), c), device_id_type=MESH)

    consts = [
        pltpu.make_async_copy(plane_ref, plane, const_sem.at[0]),
        pltpu.make_async_copy(lines_ref, lines, const_sem.at[1]),
        pltpu.make_async_copy(table_ref, table, const_sem.at[2]),
    ]
    for c in consts:
        c.start()

    row = iota((72, 512), 0)
    local = lax.rem(row, ORB)
    ident = jnp.where(row < ORB, role, nxt) * ORB + lax.rem(local, 4) * 8 + lax.div(local, 4)
    ident = jnp.where(row < 2 * ORB, ident, gi * ORB + si)
    pick = (ident == iota((72, 512), 1)).astype(BF16)
    found = dot(pick, offsets_ref[...].astype(BF16), NT)
    own_o = [found[64:65, d : d + 1].astype(I32).reshape(1, 1, 1) for d in range(3)]

    box = turn_box(box_ref[...].astype(F32).reshape(256, 128).reshape(SIDE, 8, 128), own_o, 1)
    own[:, 0] = box.reshape(16, 16, 128).astype(BF16)
    ids = slots_ref[...]
    side = iota((8, 128), 1)
    slots = jnp.full((8, 128), -1, I32)
    for k in range(6):
        at = iota((8, 128), 0) == k
        for c in range(2):
            one = jnp.broadcast_to(ids[c : c + 1, k : k + 1], (8, 128))
            slots = jnp.where(jnp.logical_and(at, side == c), one, slots)
    member = lax.rem(slots, ORB)
    spot = lax.rem(member, 8) * 4 + lax.div(member, 8)
    spot = spot + jnp.where(lax.div(slots, ORB) == gi, 0, ORB)
    spot = jnp.where(slots >= 0, spot, -1).astype(F32)
    own[:, 1] = jnp.broadcast_to(jnp.concatenate([spot, spot], 0).astype(BF16)[None], (16, 16, 128))

    pltpu.make_async_copy(own.at[q], mid.at[q], recv1).start()
    pl.semaphore_wait(entry, 61)

    @pl.loop(1, 16)
    def _(t):
        px, py, _ = rotated(x, y, core, t)
        pltpu.make_async_remote_copy(
            own.at[px * 4 + py], mid.at[q], send1, recv1, device(px, py, z, core), MESH
        ).start()

    pltpu.make_async_copy(mid, mid, recv1).wait()

    heap = mid[:, 0].astype(F32).reshape(4, 4, 2, 8, 128)
    lists = mid[:, 1].astype(F32)[:, :8].reshape(4, 4, 8, 128)
    row8, lane8 = iota((8, 128), 0), iota((8, 128), 1)
    for g in range(4):
        merged = jnp.where(lane8 < 2, lists[g, 0], 0.0)
        for j in range(1, 4):
            merged = merged + jnp.where(lax.div(lane8, 2) == j, roll(lists[g, j], 2 * j, 1), 0.0)
        spread = merged
        for t in range(1, 6):
            spread = spread + roll(merged, 8 * t, 1)
        spread = jnp.where(lax.div(lane8, 8) == row8, spread, 0.0)
        pair_out[g] = jnp.sum(spread, axis=0, keepdims=True)
        for c in range(2):
            part = heap[g, :, c].reshape(2, 16, 128).astype(BF16)
            boxes_out[g, c] = part
    sends2 = []
    for kind in range(3):
        for k in range(4):
            g = lax.rem(k + zl, 4)
            for c in range(2):
                target = lax.rem(g * 4 + zh * 2 + core + GROUPS - (1 if kind == 2 else 0), GROUPS)
                here = jnp.logical_and(target == z, core == c)
                out = pair_out.at[g] if kind == 0 else boxes_out.at[g, c]
                into = (pair_in, near_in, far_in)[kind].at[zl]
                remote = pltpu.make_async_remote_copy(
                    out, into, send2.at[kind, k, c], recv2.at[kind], device(x, y, target, c), MESH
                )
                local_copy = pltpu.make_async_copy(out, into, recv2.at[kind])
                pl.when(here)(local_copy.start)
                pl.when(jnp.logical_not(here))(remote.start)
                sends2.append((here, remote))
    pltpu.make_async_copy(own.at[pl.ds(0, 15)], own.at[pl.ds(0, 15)], send1).wait()
    pltpu.make_async_copy(pair_in, pair_in, recv2.at[0]).wait()

    lists = pair_in[...].reshape(8, 128)
    spots = [(8 * t + 2 * j) for t in range(6) for j in range(4)]
    left = jnp.concatenate([lists[:, a : a + 1] for a in spots], 0)
    right = jnp.concatenate([lists[:, a + 1 : a + 2] for a in spots], 0)
    live = left >= 0
    live_f = jnp.where(live, 1.0, 0.0)
    before = (iota((192, 192), 1) < iota((192, 192), 0)).astype(BF16)
    rank = dot(before, jnp.broadcast_to(live_f, (192, 128)).astype(BF16))[:, 0:1]
    rank = jnp.where(live, rank, -1.0)
    chosen = (jnp.broadcast_to(rank, (192, 256)) == iota((192, 256), 1).astype(F32)).astype(BF16)
    orbital = iota((192, 128), 1).astype(F32)
    pick_l = (jnp.broadcast_to(left, (192, 128)) == orbital).astype(BF16)
    pick_r = (jnp.broadcast_to(right, (192, 128)) == orbital).astype(BF16)
    one_l = dot(chosen, pick_l, TN)[:PAIRS]
    one_r = dot(chosen, pick_r, TN)[:PAIRS]
    ohl[...] = one_l
    ohr[...] = one_r
    o3 = jnp.concatenate([found[:64], jnp.zeros((64, found.shape[1]), F32)], 0)
    offs[...] = jnp.broadcast_to(dot(one_l.astype(BF16), o3.astype(BF16))[:, :3], (PAIRS, 3)).astype(I32)

    lane = iota((64, PLANE), 1)
    o = [jnp.broadcast_to(found[:64, d : d + 1], (64, PLANE)) for d in range(3)]
    code = jnp.where(rho.astype(F32) < o[0], 1.0, 0.0)
    code = code + jnp.where(lax.div(lane, SIDE).astype(F32) < o[1], 2.0, 0.0)
    code = code + jnp.where(jnp.bitwise_and(lane, SIDE - 1).astype(F32) < o[2], 4.0, 0.0)
    pltpu.make_async_copy(near_in, near_in, recv2.at[1]).wait()
    pltpu.make_async_copy(far_in, far_in, recv2.at[2]).wait()
    cells[0:256] = near_in[...].astype(F32).reshape(256, 128)
    cells[256:512] = far_in[...].astype(F32).reshape(256, 128)
    orbs = jnp.concatenate([cells[pl.ds(r, 64, stride=8), :] for r in range(8)], 1)
    both = jnp.concatenate([orbs, code], 1).astype(BF16)
    both = jnp.concatenate([both, jnp.zeros((64, 2 * PLANE), BF16)], 0)

    for b in range(PAIRS // BLOCK):
        rows = slice(b * BLOCK, (b + 1) * BLOCK)
        lv = dot(ohl[rows].astype(BF16), both)
        rv = dot(ohr[rows].astype(BF16), both)
        same = lv[:, PLANE:] == rv[:, PLANE:]
        lmv = jnp.where(same, lv[:, :PLANE], 0.0)
        rmv = jnp.where(same, rv[:, :PLANE], 0.0)
        lm[rows] = lmv
        rm[rows] = rmv
        dens = turn_rows(lmv * rmv, offs[rows, 1:2], offs[rows, 2:3], -1)
        dh[rows], dl[rows] = split(dens)

    for c in consts:
        c.wait()

    def part_of(ref, r):
        return ref.at[
            pl.ds(pl.multiple_of(lax.div(r, 8) * PART, 8), PART),
            pl.ds(pl.multiple_of(lax.rem(r, 8) * 128, 128), 128),
        ]

    for dy in (2, 1, 3, 0):
        py = lax.rem(y + dy, 4)
        cols = pl.ds(pl.multiple_of(py * 256, 256), 256)
        wh, wl = plane[0, :, cols], plane[1, :, cols]
        modes[:, cols] = dot(dh[...], wh) + dot(dl[...], wh) + dot(dh[...], wl)
        for dx in (2, 1, 3, 0):
            for dc in (1, 0):
                px, pc = lax.rem(x + dx, 4), lax.rem(core + dc, 2)
                r = px * 8 + py * 2 + pc
                if (dx, dy, dc) == (0, 0, 0):
                    pltpu.make_async_copy(part_of(modes, rho), lines_in.at[rho], recv3).start()
                else:
                    pltpu.make_async_remote_copy(
                        part_of(modes, r), lines_in.at[rho], send3, recv3, device(px, py, z, pc), MESH
                    ).start()

    pltpu.make_async_copy(lines_in, lines_in, recv3).wait()

    u, v = lax.div(rho, 8), lax.rem(rho, 8)
    scale = table[:, pl.ds(pl.multiple_of(v * 128, 128), 128)]
    scale = jnp.broadcast_to(scale[:, None, :], (SIDE, 8, 128)).reshape(256, 128)
    for j in range(PART // 8):
        rows = slice(8 * j, 8 * j + 8)
        o1 = offs[pl.ds(pl.multiple_of(u * PART, 8) + 8 * j, 8), 0:1]
        s = turn_lead(lines_in[:, rows, :], o1, -1).reshape(256, 128)
        for way in range(2):
            sh, sl = split(s)
            s = dot(lines[0, way], sh) + dot(lines[0, way], sl) + dot(lines[1, way], sh)
            if way == 0:
                s = s * scale
        lines_out[:, rows, :] = turn_lead(s.reshape(SIDE, 8, 128), o1, 1)

    pltpu.make_async_copy(lines_out.at[rho], part_of(back, rho), recv4).start()

    @pl.loop(1, 32)
    def _(t):
        px, py, pc = rotated(x, y, core, t)
        r = px * 8 + py * 2 + pc
        pltpu.make_async_remote_copy(
            lines_out.at[r], part_of(back, rho), send4, recv4, device(px, py, z, pc), MESH
        ).start()

    pltpu.make_async_copy(lines_in.at[pl.ds(0, 31)], lines_in.at[pl.ds(0, 31)], send3).wait()
    pltpu.make_async_copy(back, back, recv4).wait()

    bh, bl = split(back[...])
    dh[...] = bh
    dl[...] = bl
    for n in range(4):
        cols = slice(n * 256, (n + 1) * 256)
        wh, wl = plane[0, cols, :], plane[1, cols, :]
        modes[:, cols] = dot(dh[...], wh, NT) + dot(dl[...], wh, NT) + dot(dh[...], wl, NT)

    for b in range(PAIRS // BLOCK):
        rows = slice(b * BLOCK, (b + 1) * BLOCK)
        pot = turn_rows(modes[rows], offs[rows, 1:2], offs[rows, 2:3], 1)
        dh[rows], dl[rows] = split(pot * lm[rows])
        eh[rows], el[rows] = split(pot * rm[rows])
    pick_f = ohr[:, ORB : 2 * ORB].astype(BF16)
    far_field[...] = dot(pick_f, dh[...], TN) + dot(pick_f, dl[...], TN)

    far_copy = pltpu.make_async_remote_copy(far_field, prev_field, send5, recv5, device(x, y, nxt, core), MESH)
    far_copy.start()
    pick_f = ohr[:, 0:ORB].astype(BF16)
    total = dot(pick_f, dh[...], TN) + dot(pick_f, dl[...], TN)
    pick_f = ohl[:, 0:ORB].astype(BF16)
    total = total + dot(pick_f, eh[...], TN) + dot(pick_f, el[...], TN)
    framed = jnp.where(code[:ORB] == code[0:1], orbs[:ORB], 0.0)
    perm_row = iota((128, ORB), 0)
    perm = (lax.rem(perm_row, 8) * 4 + lax.div(perm_row, 8) == iota((128, ORB), 1)) & (perm_row < ORB)
    framed = dot(perm.astype(BF16), framed.astype(BF16)).astype(BF16)
    far_copy.wait_recv()
    summed = total + prev_field[...]
    for r in range(8):
        tiles[pl.ds(r, ORB, stride=8), :] = summed[:, r * 128 : (r + 1) * 128]
    send6[...] = tiles[...].reshape(8, 4, 8, 128)

    home_x, home_zh, home_c = lax.div(role, 4), lax.rem(lax.div(role, 2), 2), lax.rem(role, 2)
    sends6 = []

    def along_z(out_of, into, send, recv):
        for t in range(8):
            k = lax.rem(zl + t, 8)
            target = home_zh * 8 + k
            here = jnp.logical_and(target == z, home_c == core)
            remote = pltpu.make_async_remote_copy(
                out_of.at[k], into, send.at[t], recv, device(x, y, target, home_c), MESH
            )
            local_copy = pltpu.make_async_copy(out_of.at[k], into, recv)
            pl.when(here)(local_copy.start)
            pl.when(jnp.logical_not(here))(remote.start)
            sends6.append((here, remote))

    along_z(send6, mid6.at[home_x, :, core], send6s, recv6.at[home_x])
    framed_field = jnp.where(code[:ORB] == code[0:1], summed, 0.0).astype(BF16)
    gp[...] = dot(framed_field, framed, NT)
    packed = jnp.zeros((8, 128), F32)
    for j in range(4):
        packed = jnp.where(lax.div(lane8, ORB) == j, roll(gp[pl.ds(j, 8, stride=4), :], ORB * j, 1), packed)
    for k in range(8):
        gram_out[k] = packed[k : k + 1]
    along_z(gram_out, gram_mid.at[home_x, core], send6g, recv6g)

    for g in range(4):
        pltpu.make_async_copy(mid6.at[g], mid6.at[g], recv6.at[g]).wait()
        for dj in (2, 1, 3, 0):
            j = lax.rem(y + dj, 4)
            out = mid6.at[g, j]
            remote = pltpu.make_async_remote_copy(out, fin.at[q], send7s, recv7, device(g, j, z, core), MESH)
            if dj:
                remote.start()
            else:
                pl.when(x == g)(pltpu.make_async_copy(out, fin.at[q], recv7).start)
                pl.when(x != g)(remote.start)
    pltpu.make_async_copy(gram_mid, gram_mid, recv6g).wait()
    for g in range(4):
        gram_fwd[g] = gram_mid[g, 0] + gram_mid[g, 1]
    gram_fin[q] = gram_fwd[x]

    @pl.loop(1, 16)
    def _(t):
        px, py, _ = rotated(x, y, core, t)
        pltpu.make_async_remote_copy(
            gram_fwd.at[px], gram_fin.at[q], send7g, recv7g, device(px, py, z, core), MESH
        ).start()

    pltpu.make_async_copy(fin, fin, recv7).wait()
    result = turn_box(fin[...].reshape(SIDE, 8, 128), own_o, -1)
    field_ref[...] = result.reshape(256, 128)
    pltpu.make_async_copy(gram_fin.at[pl.ds(0, 15)], gram_fin.at[pl.ds(0, 15)], recv7g).wait()
    gram_row = gram_fin[0]
    for k in range(1, 16):
        gram_row = gram_row + gram_fin[k]
    gram_row = jnp.broadcast_to(gram_row, (8, 128))
    picked = gram_row
    for j in range(1, 4):
        picked = jnp.where(jnp.broadcast_to(y, (8, 128)) == j, roll(gram_row, -ORB * j, 1), picked)
    gram_ref[...] = picked[0:1] * (1.0 / math.sqrt(CELLS))

    for here, remote in sends2 + sends6:
        pl.when(jnp.logical_not(here))(remote.wait_send)
    pltpu.make_async_copy(lines_in.at[pl.ds(0, 31)], lines_in.at[pl.ds(0, 31)], send4).wait()
    far_copy.wait_send()
    pltpu.make_async_copy(fin.at[pl.ds(0, 15)], fin.at[pl.ds(0, 15)], send7s).wait()
    pltpu.make_async_copy(gram_fin.at[pl.ds(0, 15)], gram_fin.at[pl.ds(0, 15)], send7g).wait()


def on_device(orbitals, offsets, slot_pairs):
    plane_c, lines_c, table_c = constants()
    vmem = pl.BlockSpec(memory_space=pltpu.VMEM)
    hbm = pl.BlockSpec(memory_space=pltpu.HBM)
    dma = pltpu.SemaphoreType.DMA
    scratch = [
        pltpu.VMEM((2, PLANE, PLANE), BF16),
        pltpu.VMEM((2, 2, 256, 256), BF16),
        pltpu.VMEM((SIDE, PLANE), F32),
        pltpu.VMEM((16, 2, 16, 128), BF16),
        pltpu.VMEM((16, 2, 16, 128), BF16),
        pltpu.VMEM((4, 1, 128), F32),
        pltpu.VMEM((4, 2, 2, 16, 128), BF16),
        pltpu.VMEM((8, 1, 128), F32),
        pltpu.VMEM((8, 2, 16, 128), BF16),
        pltpu.VMEM((8, 2, 16, 128), BF16),
        pltpu.VMEM((512, 128), F32),
        pltpu.VMEM((PAIRS, 128), F32),
        pltpu.VMEM((PAIRS, 128), F32),
        pltpu.VMEM((PAIRS, 3), I32),
        pltpu.VMEM((PAIRS, PLANE), F32),
        pltpu.VMEM((PAIRS, PLANE), F32),
        pltpu.VMEM((PAIRS, PLANE), BF16),
        pltpu.VMEM((PAIRS, PLANE), BF16),
        pltpu.VMEM((PAIRS, PLANE), BF16),
        pltpu.VMEM((PAIRS, PLANE), BF16),
        pltpu.VMEM((PAIRS, PLANE), F32),
        pltpu.VMEM((32, PART, 128), F32),
        pltpu.VMEM((32, PART, 128), F32),
        pltpu.VMEM((PAIRS, PLANE), F32),
        pltpu.VMEM((ORB, PLANE), F32),
        pltpu.VMEM((ORB, PLANE), F32),
        pltpu.VMEM((256, 128), F32),
        pltpu.VMEM((ORB, 128), F32),
        pltpu.VMEM((8, 4, 8, 128), F32),
        pltpu.VMEM((4, 4, 2, 8, 128), F32),
        pltpu.VMEM((16, 2, 8, 128), F32),
        pltpu.VMEM((8, 1, 128), F32),
        pltpu.VMEM((4, 2, 1, 128), F32),
        pltpu.VMEM((4, 1, 128), F32),
        pltpu.VMEM((16, 1, 128), F32),
        dma((3,)),
        dma, dma,
        dma((3, 4, 2)), dma((3,)),
        dma, dma,
        dma, dma,
        dma, dma,
        dma((8,)), dma((4,)), dma((8,)), dma,
        dma, dma, dma, dma,
    ]
    field, gram = pl.pallas_call(
        kernel,
        out_shape=(jax.ShapeDtypeStruct((256, 128), F32), jax.ShapeDtypeStruct((1, 128), F32)),
        in_specs=[vmem, vmem, vmem, hbm, hbm, hbm],
        out_specs=(vmem, vmem),
        scratch_shapes=scratch,
        compiler_params=pltpu.CompilerParams(has_side_effects=True, collective_id=1, vmem_limit_bytes=63 * 2**20),
    )(
        orbitals,
        offsets.T,
        slot_pairs.T,
        jnp.asarray(plane_c),
        jnp.asarray(lines_c),
        jnp.asarray(table_c),
    )
    return field.reshape(1, CELLS), gram[0, :ORB].reshape(1, ORB, 1)


def solution(mesh):
    return jax.shard_map(
        on_device,
        mesh=mesh,
        in_specs=(P(("grp", "slab"), None), P(), P(("grp", "slab"), None)),
        out_specs=(P(("grp", "slab"), None), P("grp", None, "slab")),
        check_vma=False,
    )
```

```python
import math

import jax
import jax.numpy as jnp
import numpy as np
from jax import lax
from jax.experimental import pallas as pl
from jax.experimental.pallas import tpu as pltpu
from jax.sharding import PartitionSpec as P

SIDE = 32
PLANE = SIDE * SIDE
CELLS = SIDE * PLANE
CHEB = 6
GROUPS = 16
ORB = 32
PAIRS = 160
PARTS = ((0, 24), (96, 16))
BLOCK = 32
F32, BF16, I32 = jnp.float32, jnp.bfloat16, jnp.int32
MESH = pl.DeviceIdType.MESH

NN = (((1,), (0,)), ((), ()))
NT = (((1,), (1,)), ((), ()))
TN = (((0,), (0,)), ((), ()))


def operator_1d():
    weights = {0: -49.0 / 18.0, 1: 1.5, 2: -0.15, 3: 1.0 / 90.0}
    a = np.zeros((SIDE, SIDE))
    for i in range(SIDE):
        for j in range(SIDE):
            a[i, j] = -weights.get(abs(i - j), 0.0)
    return a


def eigen(a):
    a, n = a.copy(), a.shape[0]
    v = np.eye(n)
    for _ in range(10):
        for p in range(n - 1):
            for q in range(p + 1, n):
                if abs(a[p, q]) < 1e-18:
                    continue
                theta = (a[q, q] - a[p, p]) / (2.0 * a[p, q])
                t = (1.0 if theta >= 0 else -1.0) / (abs(theta) + math.sqrt(theta * theta + 1.0))
                c = 1.0 / math.sqrt(t * t + 1.0)
                s = t * c
                ap, aq = a[:, p].copy(), a[:, q].copy()
                a[:, p], a[:, q] = c * ap - s * aq, s * ap + c * aq
                ap, aq = a[p].copy(), a[q].copy()
                a[p], a[q] = c * ap - s * aq, s * ap + c * aq
                vp, vq = v[:, p].copy(), v[:, q].copy()
                v[:, p], v[:, q] = c * vp - s * vq, s * vp + c * vq
    return np.diag(a).copy(), v


def polynomial(lam):
    low, high = 3.0 * (math.pi / (SIDE + 1)) ** 2, 18.2
    mid, half = 0.5 * (high + low), 0.5 * (high - low)
    alpha, beta = 1.0 / mid, 0.0
    x, res, p = np.zeros_like(lam), np.ones_like(lam), np.zeros_like(lam)
    for k in range(1, CHEB + 1):
        if k > 1:
            beta = 0.5 * (half * alpha) ** 2 if k == 2 else (0.5 * half * alpha) ** 2
            alpha = 1.0 / (mid - beta / alpha)
        p = res + beta * p
        x = x + alpha * p
        res = res - alpha * lam * p
    return x


def halves(a):
    high = a.astype(BF16)
    low = (a - high.astype(np.float64)).astype(BF16)
    return np.stack([high, low])


def constants():
    lam, q = eigen(operator_1d())
    plane = halves(np.kron(q, q))
    lines = halves(np.stack([np.kron(q.T, np.eye(8)), np.kron(q, np.eye(8))]))
    total = lam[:, None, None] + lam[None, :, None] + lam[None, None, :]
    table = polynomial(total).reshape(SIDE, PLANE).astype(np.float32)
    return plane, lines, table


def iota(shape, dim):
    return lax.broadcasted_iota(I32, shape, dim)


def roll(x, n, axis):
    n %= x.shape[axis]
    return pltpu.roll(x, n, axis) if n else x


def lead(x, n):
    n %= x.shape[0]
    return jnp.concatenate([x[x.shape[0] - n :], x[: x.shape[0] - n]], 0) if n else x


def bit(o, b):
    return jnp.bitwise_and(jnp.right_shift(o, b), 1) > 0


def turn_rows(x, o2, o3, sign):
    third = jnp.bitwise_and(iota(x.shape, 1), SIDE - 1)
    b2 = jnp.broadcast_to(o2, x.shape)
    b3 = jnp.broadcast_to(o3, x.shape)
    for b in range(4):
        n = 1 << b
        x = jnp.where(bit(b2, b), roll(x, sign * SIDE * n, 1), x)
        inside = third >= n if sign > 0 else third < SIDE - n
        y = jnp.where(inside, roll(x, sign * n, 1), roll(x, sign * (n - SIDE), 1))
        x = jnp.where(bit(b3, b), y, x)
    return x


def turn_box(x, o, sign):
    o1, o2, o3 = (jnp.broadcast_to(v, x.shape) for v in o)
    lane = iota(x.shape, 2)
    third = jnp.bitwise_and(lane, SIDE - 1)
    for b in range(4):
        n = 1 << b
        x = jnp.where(bit(o1, b), lead(x, sign * n), x)
        if b < 2:
            y = roll(x, sign * SIDE * n, 2)
            kept = lane >= SIDE * n if sign > 0 else lane < 128 - SIDE * n
            y = jnp.where(kept, y, roll(y, sign, 1))
        else:
            y = roll(x, sign * n // 4, 1)
        x = jnp.where(bit(o2, b), y, x)
        inside = third >= n if sign > 0 else third < SIDE - n
        y = jnp.where(inside, roll(x, sign * n, 2), roll(x, sign * (n - SIDE), 2))
        x = jnp.where(bit(o3, b), y, x)
    return x


def turn_lead(x, o1, sign):
    o = jnp.broadcast_to(o1, x.shape[1:])[None]
    for b in range(4):
        x = jnp.where(bit(o, b), lead(x, sign << b if sign > 0 else -(1 << b)), x)
    return x


def split(x):
    high = x.astype(BF16)
    return high, (x - high.astype(F32)).astype(BF16)


def dot(a, b, dims=NN):
    return lax.dot_general(a, b, dims, preferred_element_type=F32)


def rotated(x, y, core, t):
    m = lax.rem(t * 5, 16)
    return (
        lax.rem(x + lax.div(m, 4), 4),
        lax.rem(y + lax.rem(m, 4), 4),
        lax.rem(core + lax.div(t, 16), 2),
    )


def device(x, y, z, c):
    return x * 4 + lax.div(z, 8) * 2 + c, y * 8 + lax.rem(z, 8)


def kernel(
    box_ref, offsets_ref, slots_ref, plane_ref, lines_ref, table_ref,
    field_ref, gram_ref,
    plane, lines, table, own, mid, pair_out, boxes_out, pair_in, near_in, far_in, cells,
    ohl, ohr, offs, lm, rm, dh, dl, eh, el, modes, in_a, in_b, out_a, out_b, back, pots,
    field, far_field, prev_field, tiles, gp, send6, mid6, fin, gram_out, gram_mid, gram_fwd, gram_fin,
    const_sem, send1, recv1, send2, recv2, send3, recv3, send4, recv4, send5, recv5,
    send6s, recv6, send6g, recv6g, send7s, recv7, send7g, recv7g,
):
    gi, si = lax.axis_index("grp"), lax.axis_index("slab")
    x, zh, core = lax.div(gi, 4), lax.rem(lax.div(gi, 2), 2), lax.rem(gi, 2)
    y, zl = lax.div(si, 8), lax.rem(si, 8)
    z = zh * 8 + zl
    q = x * 4 + y
    rho = q * 2 + core
    role = z
    nxt = lax.rem(role + 1, GROUPS)

    entry = pltpu.get_barrier_semaphore()

    @pl.loop(1, 32)
    def _(t):
        peer = rotated(x, y, core, t)
        pl.semaphore_signal(entry, 1, device_id=device(peer[0], peer[1], z, peer[2]), device_id_type=MESH)

    @pl.loop(1, 16)
    def _(t):
        for c in range(2):
            pl.semaphore_signal(entry, 1, device_id=device(x, y, lax.rem(z + t, 16), c), device_id_type=MESH)

    consts = [
        pltpu.make_async_copy(plane_ref, plane, const_sem.at[0]),
        pltpu.make_async_copy(lines_ref, lines, const_sem.at[1]),
        pltpu.make_async_copy(table_ref, table, const_sem.at[2]),
    ]
    for c in consts:
        c.start()

    row = iota((72, 512), 0)
    local = lax.rem(row, ORB)
    ident = jnp.where(row < ORB, role, nxt) * ORB + lax.rem(local, 4) * 8 + lax.div(local, 4)
    ident = jnp.where(row < 2 * ORB, ident, gi * ORB + si)
    pick = (ident == iota((72, 512), 1)).astype(BF16)
    found = dot(pick, offsets_ref[...].astype(BF16), NT)
    own_o = [found[64:65, d : d + 1].astype(I32).reshape(1, 1, 1) for d in range(3)]

    box = turn_box(box_ref[...].astype(F32).reshape(256, 128).reshape(SIDE, 8, 128), own_o, 1)
    own[:, 0] = box.reshape(16, 16, 128).astype(BF16)
    ids = slots_ref[...]
    side = iota((8, 128), 1)
    slots = jnp.full((8, 128), -1, I32)
    for k in range(6):
        at = iota((8, 128), 0) == k
        for c in range(2):
            one = jnp.broadcast_to(ids[c : c + 1, k : k + 1], (8, 128))
            slots = jnp.where(jnp.logical_and(at, side == c), one, slots)
    member = lax.rem(slots, ORB)
    spot = lax.rem(member, 8) * 4 + lax.div(member, 8)
    spot = spot + jnp.where(lax.div(slots, ORB) == gi, 0, ORB)
    spot = jnp.where(slots >= 0, spot, -1).astype(F32)
    own[:, 1] = jnp.broadcast_to(jnp.concatenate([spot, spot], 0).astype(BF16)[None], (16, 16, 128))

    pltpu.make_async_copy(own.at[q], mid.at[q], recv1).start()
    pl.semaphore_wait(entry, 61)

    @pl.loop(1, 16)
    def _(t):
        px, py, _ = rotated(x, y, core, t)
        pltpu.make_async_remote_copy(
            own.at[px * 4 + py], mid.at[q], send1, recv1, device(px, py, z, core), MESH
        ).start()

    pltpu.make_async_copy(mid, mid, recv1).wait()

    heap = mid[:, 0].astype(F32).reshape(4, 4, 2, 8, 128)
    lists = mid[:, 1].astype(F32)[:, :8].reshape(4, 4, 8, 128)
    row8, lane8 = iota((8, 128), 0), iota((8, 128), 1)
    for g in range(4):
        merged = jnp.where(lane8 < 2, lists[g, 0], 0.0)
        for j in range(1, 4):
            merged = merged + jnp.where(lax.div(lane8, 2) == j, roll(lists[g, j], 2 * j, 1), 0.0)
        spread = merged
        for t in range(1, 6):
            spread = spread + roll(merged, 8 * t, 1)
        spread = jnp.where(lax.div(lane8, 8) == row8, spread, 0.0)
        pair_out[g] = jnp.sum(spread, axis=0, keepdims=True)
        for c in range(2):
            part = heap[g, :, c].reshape(2, 16, 128).astype(BF16)
            boxes_out[g, c] = part
    sends2 = []
    for kind in range(3):
        for k in range(4):
            g = lax.rem(k + zl, 4)
            for c in range(2):
                target = lax.rem(g * 4 + zh * 2 + core + GROUPS - (1 if kind == 2 else 0), GROUPS)
                here = jnp.logical_and(target == z, core == c)
                out = pair_out.at[g] if kind == 0 else boxes_out.at[g, c]
                into = (pair_in, near_in, far_in)[kind].at[zl]
                remote = pltpu.make_async_remote_copy(
                    out, into, send2.at[kind, k, c], recv2.at[kind], device(x, y, target, c), MESH
                )
                local_copy = pltpu.make_async_copy(out, into, recv2.at[kind])
                pl.when(here)(local_copy.start)
                pl.when(jnp.logical_not(here))(remote.start)
                sends2.append((here, remote))
    pltpu.make_async_copy(own.at[pl.ds(0, 15)], own.at[pl.ds(0, 15)], send1).wait()
    pltpu.make_async_copy(pair_in, pair_in, recv2.at[0]).wait()

    lists = pair_in[...].reshape(8, 128)
    spots = [(8 * t + 2 * j) for t in range(6) for j in range(4)]
    left = jnp.concatenate([lists[:, a : a + 1] for a in spots], 0)
    right = jnp.concatenate([lists[:, a + 1 : a + 2] for a in spots], 0)
    live = left >= 0
    live_f = jnp.where(live, 1.0, 0.0)
    before = (iota((192, 192), 1) < iota((192, 192), 0)).astype(BF16)
    rank = dot(before, jnp.broadcast_to(live_f, (192, 128)).astype(BF16))[:, 0:1]
    rank = jnp.where(live, rank, -1.0)
    chosen = (jnp.broadcast_to(rank, (192, 256)) == iota((192, 256), 1).astype(F32)).astype(BF16)
    orbital = iota((192, 128), 1).astype(F32)
    pick_l = (jnp.broadcast_to(left, (192, 128)) == orbital).astype(BF16)
    pick_r = (jnp.broadcast_to(right, (192, 128)) == orbital).astype(BF16)
    one_l = dot(chosen, pick_l, TN)[:PAIRS]
    one_r = dot(chosen, pick_r, TN)[:PAIRS]
    ohl[...] = one_l
    ohr[...] = one_r
    o3 = jnp.concatenate([found[:64], jnp.zeros((64, found.shape[1]), F32)], 0)
    offs[...] = jnp.broadcast_to(dot(one_l.astype(BF16), o3.astype(BF16))[:, :3], (PAIRS, 3)).astype(I32)

    lane = iota((64, PLANE), 1)
    o = [jnp.broadcast_to(found[:64, d : d + 1], (64, PLANE)) for d in range(3)]
    code = jnp.where(rho.astype(F32) < o[0], 1.0, 0.0)
    code = code + jnp.where(lax.div(lane, SIDE).astype(F32) < o[1], 2.0, 0.0)
    code = code + jnp.where(jnp.bitwise_and(lane, SIDE - 1).astype(F32) < o[2], 4.0, 0.0)
    pltpu.make_async_copy(near_in, near_in, recv2.at[1]).wait()
    pltpu.make_async_copy(far_in, far_in, recv2.at[2]).wait()
    cells[0:256] = near_in[...].astype(F32).reshape(256, 128)
    cells[256:512] = far_in[...].astype(F32).reshape(256, 128)
    orbs = jnp.concatenate([cells[pl.ds(r, 64, stride=8), :] for r in range(8)], 1)
    both = jnp.concatenate([orbs, code], 1).astype(BF16)
    both = jnp.concatenate([both, jnp.zeros((64, 2 * PLANE), BF16)], 0)

    for b in range(PAIRS // BLOCK):
        rows = slice(b * BLOCK, (b + 1) * BLOCK)
        lv = dot(ohl[rows].astype(BF16), both)
        rv = dot(ohr[rows].astype(BF16), both)
        same = lv[:, PLANE:] == rv[:, PLANE:]
        lmv = jnp.where(same, lv[:, :PLANE], 0.0)
        rmv = jnp.where(same, rv[:, :PLANE], 0.0)
        lm[rows] = lmv
        rm[rows] = rmv
        dens = turn_rows(lmv * rmv, offs[rows, 1:2], offs[rows, 2:3], -1)
        dh[rows], dl[rows] = split(dens)

    for c in consts:
        c.wait()

    def part_of(ref, r, part):
        base, size = PARTS[part]
        return ref.at[
            pl.ds(pl.multiple_of(base + lax.div(r, 8) * size, 8), size),
            pl.ds(pl.multiple_of(lax.rem(r, 8) * 128, 128), 128),
        ]

    lines_in, lines_out = (in_a, in_b), (out_a, out_b)
    for part, (base, size) in enumerate(PARTS):
        rows = slice(base, base + 4 * size)
        landing = lines_in[part].at[rho]
        for dy in (2, 1, 3, 0):
            py = lax.rem(y + dy, 4)
            cols = pl.ds(pl.multiple_of(py * 256, 256), 256)
            wh, wl = plane[0, :, cols], plane[1, :, cols]
            modes[rows, cols] = dot(dh[rows], wh) + dot(dl[rows], wh) + dot(dh[rows], wl)
            for dx in (2, 1, 3, 0):
                for dc in (1, 0):
                    px, pc = lax.rem(x + dx, 4), lax.rem(core + dc, 2)
                    out = part_of(modes, px * 8 + py * 2 + pc, part)
                    if (dx, dy, dc) == (0, 0, 0):
                        pltpu.make_async_copy(out, landing, recv3.at[part]).start()
                    else:
                        pltpu.make_async_remote_copy(
                            out, landing, send3.at[part], recv3.at[part], device(px, py, z, pc), MESH
                        ).start()

    u, v = lax.div(rho, 8), lax.rem(rho, 8)
    scale = table[:, pl.ds(pl.multiple_of(v * 128, 128), 128)]
    scale = jnp.broadcast_to(scale[:, None, :], (SIDE, 8, 128)).reshape(256, 128)
    for part, (base, size) in enumerate(PARTS):
        source, result = lines_in[part], lines_out[part]
        pltpu.make_async_copy(source, source, recv3.at[part]).wait()
        for j in range(size // 8):
            rows = slice(8 * j, 8 * j + 8)
            o1 = offs[pl.ds(pl.multiple_of(base + u * size + 8 * j, 8), 8), 0:1]
            s = turn_lead(source[:, rows, :], o1, -1).reshape(256, 128)
            for way in range(2):
                sh, sl = split(s)
                s = dot(lines[0, way], sh) + dot(lines[0, way], sl) + dot(lines[1, way], sh)
                if way == 0:
                    s = s * scale
            result[:, rows, :] = turn_lead(s.reshape(SIDE, 8, 128), o1, 1)

        landing = part_of(back, rho, part)
        pltpu.make_async_copy(result.at[rho], landing, recv4.at[part]).start()

        @pl.loop(1, 32)
        def _(t):
            px, py, pc = rotated(x, y, core, t)
            r = px * 8 + py * 2 + pc
            pltpu.make_async_remote_copy(
                result.at[r], landing, send4.at[part], recv4.at[part], device(px, py, z, pc), MESH
            ).start()

    for part, (base, size) in enumerate(PARTS):
        rows = slice(base, base + 4 * size)
        arrived = back.at[pl.ds(base, 4 * size)]
        pltpu.make_async_copy(arrived, arrived, recv4.at[part]).wait()
        dh[rows], dl[rows] = split(back[rows])
        for n in range(4):
            cols = slice(n * 256, (n + 1) * 256)
            wh, wl = plane[0, cols, :], plane[1, cols, :]
            pots[rows, cols] = dot(dh[rows], wh, NT) + dot(dl[rows], wh, NT) + dot(dh[rows], wl, NT)
        for b in range(4 * size // BLOCK):
            rows = slice(base + b * BLOCK, base + (b + 1) * BLOCK)
            pot = turn_rows(pots[rows], offs[rows, 1:2], offs[rows, 2:3], 1)
            dh[rows], dl[rows] = split(pot * lm[rows])
            eh[rows], el[rows] = split(pot * rm[rows])
    pick_f = ohr[:, ORB : 2 * ORB].astype(BF16)
    far_field[...] = dot(pick_f, dh[...], TN) + dot(pick_f, dl[...], TN)

    far_copies = []
    for t in range(4):
        k = lax.rem(lax.div(lax.rem(zl + 1, 8), 2) + t, 4)
        rows = pl.ds(pl.multiple_of(8 * k, 8), 8)
        far_copies.append(
            pltpu.make_async_remote_copy(
                far_field.at[rows], prev_field.at[rows], send5.at[t], recv5.at[k], device(x, y, nxt, core), MESH
            )
        )
        far_copies[-1].start()
    pick_f = ohr[:, 0:ORB].astype(BF16)
    total = dot(pick_f, dh[...], TN) + dot(pick_f, dl[...], TN)
    pick_f = ohl[:, 0:ORB].astype(BF16)
    field[...] = total + dot(pick_f, eh[...], TN) + dot(pick_f, el[...], TN)
    framed = jnp.where(code[:ORB] == code[0:1], orbs[:ORB], 0.0)
    perm_row = iota((128, ORB), 0)
    perm = (lax.rem(perm_row, 8) * 4 + lax.div(perm_row, 8) == iota((128, ORB), 1)) & (perm_row < ORB)
    framed = dot(perm.astype(BF16), framed.astype(BF16)).astype(BF16)
    home_x, home_zh, home_c = lax.div(role, 4), lax.rem(lax.div(role, 2), 2), lax.rem(role, 2)
    sends6 = []

    def along_z(out, k, into, send, recv):
        target = home_zh * 8 + k
        here = jnp.logical_and(target == z, home_c == core)
        remote = pltpu.make_async_remote_copy(out, into, send, recv, device(x, y, target, home_c), MESH)
        pl.when(here)(pltpu.make_async_copy(out, into, recv).start)
        pl.when(jnp.logical_not(here))(remote.start)
        sends6.append((here, remote))

    for t in range(4):
        k = lax.rem(lax.div(zl, 2) + t, 4)
        rows = pl.ds(pl.multiple_of(8 * k, 8), 8)
        arrived = prev_field.at[rows]
        pltpu.make_async_copy(arrived, arrived, recv5.at[k]).wait()
        summed = field[rows] + prev_field[rows]
        field[rows] = summed
        for r in range(8):
            tiles[pl.ds(r, 8, stride=8), :] = summed[:, r * 128 : (r + 1) * 128]
        for half in range(2):
            send6[2 * k + half] = tiles[32 * half : 32 * half + 32].reshape(4, 8, 128)
            along_z(
                send6.at[2 * k + half], 2 * k + half, mid6.at[home_x, :, core],
                send6s.at[2 * t + half], recv6.at[home_x],
            )
    framed_field = jnp.where(code[:ORB] == code[0:1], field[...], 0.0).astype(BF16)
    gp[...] = dot(framed_field, framed, NT)
    packed = jnp.zeros((8, 128), F32)
    for j in range(4):
        packed = jnp.where(lax.div(lane8, ORB) == j, roll(gp[pl.ds(j, 8, stride=4), :], ORB * j, 1), packed)
    for k in range(8):
        gram_out[k] = packed[k : k + 1]
    for t in range(8):
        k = lax.rem(zl + t, 8)
        along_z(gram_out.at[k], k, gram_mid.at[home_x, core], send6g.at[t], recv6g)

    for g in range(4):
        pltpu.make_async_copy(mid6.at[g], mid6.at[g], recv6.at[g]).wait()
        for dj in (2, 1, 3, 0):
            j = lax.rem(y + dj, 4)
            out = mid6.at[g, j]
            remote = pltpu.make_async_remote_copy(out, fin.at[q], send7s, recv7, device(g, j, z, core), MESH)
            if dj:
                remote.start()
            else:
                pl.when(x == g)(pltpu.make_async_copy(out, fin.at[q], recv7).start)
                pl.when(x != g)(remote.start)
    pltpu.make_async_copy(gram_mid, gram_mid, recv6g).wait()
    for g in range(4):
        gram_fwd[g] = gram_mid[g, 0] + gram_mid[g, 1]
    gram_fin[q] = gram_fwd[x]

    @pl.loop(1, 16)
    def _(t):
        px, py, _ = rotated(x, y, core, t)
        pltpu.make_async_remote_copy(
            gram_fwd.at[px], gram_fin.at[q], send7g, recv7g, device(px, py, z, core), MESH
        ).start()

    pltpu.make_async_copy(fin, fin, recv7).wait()
    result = turn_box(fin[...].reshape(SIDE, 8, 128), own_o, -1)
    field_ref[...] = result.reshape(256, 128)
    pltpu.make_async_copy(gram_fin.at[pl.ds(0, 15)], gram_fin.at[pl.ds(0, 15)], recv7g).wait()
    gram_row = gram_fin[0]
    for k in range(1, 16):
        gram_row = gram_row + gram_fin[k]
    gram_row = jnp.broadcast_to(gram_row, (8, 128))
    picked = gram_row
    for j in range(1, 4):
        picked = jnp.where(jnp.broadcast_to(y, (8, 128)) == j, roll(gram_row, -ORB * j, 1), picked)
    gram_ref[...] = picked[0:1] * (1.0 / math.sqrt(CELLS))

    for here, remote in sends2 + sends6:
        pl.when(jnp.logical_not(here))(remote.wait_send)
    for part in range(2):
        sent = lines_in[part].at[pl.ds(0, 31)]
        pltpu.make_async_copy(sent, sent, send3.at[part]).wait()
        pltpu.make_async_copy(sent, sent, send4.at[part]).wait()
    for far_copy in far_copies:
        far_copy.wait_send()
    pltpu.make_async_copy(fin.at[pl.ds(0, 15)], fin.at[pl.ds(0, 15)], send7s).wait()
    pltpu.make_async_copy(gram_fin.at[pl.ds(0, 15)], gram_fin.at[pl.ds(0, 15)], send7g).wait()


def on_device(orbitals, offsets, slot_pairs):
    plane_c, lines_c, table_c = constants()
    vmem = pl.BlockSpec(memory_space=pltpu.VMEM)
    hbm = pl.BlockSpec(memory_space=pltpu.HBM)
    dma = pltpu.SemaphoreType.DMA
    scratch = [
        pltpu.VMEM((2, PLANE, PLANE), BF16),
        pltpu.VMEM((2, 2, 256, 256), BF16),
        pltpu.VMEM((SIDE, PLANE), F32),
        pltpu.VMEM((16, 2, 16, 128), BF16),
        pltpu.VMEM((16, 2, 16, 128), BF16),
        pltpu.VMEM((4, 1, 128), F32),
        pltpu.VMEM((4, 2, 2, 16, 128), BF16),
        pltpu.VMEM((8, 1, 128), F32),
        pltpu.VMEM((8, 2, 16, 128), BF16),
        pltpu.VMEM((8, 2, 16, 128), BF16),
        pltpu.VMEM((512, 128), F32),
        pltpu.VMEM((PAIRS, 128), F32),
        pltpu.VMEM((PAIRS, 128), F32),
        pltpu.VMEM((PAIRS, 3), I32),
        pltpu.VMEM((PAIRS, PLANE), F32),
        pltpu.VMEM((PAIRS, PLANE), F32),
        pltpu.VMEM((PAIRS, PLANE), BF16),
        pltpu.VMEM((PAIRS, PLANE), BF16),
        pltpu.VMEM((PAIRS, PLANE), BF16),
        pltpu.VMEM((PAIRS, PLANE), BF16),
        pltpu.VMEM((PAIRS, PLANE), F32),
        pltpu.VMEM((32, PARTS[0][1], 128), F32),
        pltpu.VMEM((32, PARTS[1][1], 128), F32),
        pltpu.VMEM((32, PARTS[0][1], 128), F32),
        pltpu.VMEM((32, PARTS[1][1], 128), F32),
        pltpu.VMEM((PAIRS, PLANE), F32),
        pltpu.VMEM((PAIRS, PLANE), F32),
        pltpu.VMEM((ORB, PLANE), F32),
        pltpu.VMEM((ORB, PLANE), F32),
        pltpu.VMEM((ORB, PLANE), F32),
        pltpu.VMEM((64, 128), F32),
        pltpu.VMEM((ORB, 128), F32),
        pltpu.VMEM((8, 4, 8, 128), F32),
        pltpu.VMEM((4, 4, 2, 8, 128), F32),
        pltpu.VMEM((16, 2, 8, 128), F32),
        pltpu.VMEM((8, 1, 128), F32),
        pltpu.VMEM((4, 2, 1, 128), F32),
        pltpu.VMEM((4, 1, 128), F32),
        pltpu.VMEM((16, 1, 128), F32),
        dma((3,)),
        dma, dma,
        dma((3, 4, 2)), dma((3,)),
        dma((2,)), dma((2,)),
        dma((2,)), dma((2,)),
        dma((4,)), dma((4,)),
        dma((8,)), dma((4,)), dma((8,)), dma,
        dma, dma, dma, dma,
    ]
    field, gram = pl.pallas_call(
        kernel,
        out_shape=(jax.ShapeDtypeStruct((256, 128), F32), jax.ShapeDtypeStruct((1, 128), F32)),
        in_specs=[vmem, vmem, vmem, hbm, hbm, hbm],
        out_specs=(vmem, vmem),
        scratch_shapes=scratch,
        compiler_params=pltpu.CompilerParams(has_side_effects=True, collective_id=1, vmem_limit_bytes=63 * 2**20),
    )(
        orbitals,
        offsets.T,
        slot_pairs.T,
        jnp.asarray(plane_c),
        jnp.asarray(lines_c),
        jnp.asarray(table_c),
    )
    return field.reshape(1, CELLS), gram[0, :ORB].reshape(1, ORB, 1)


def solution(mesh):
    return jax.shard_map(
        on_device,
        mesh=mesh,
        in_specs=(P(("grp", "slab"), None), P(), P(("grp", "slab"), None)),
        out_specs=(P(("grp", "slab"), None), P("grp", None, "slab")),
        check_vma=False,
    )
```

```python
import math

import jax
import jax.numpy as jnp
import numpy as np
from jax import lax
from jax.experimental import pallas as pl
from jax.experimental.pallas import tpu as pltpu
from jax.sharding import PartitionSpec as P

SIDE = 32
PLANE = SIDE * SIDE
CELLS = SIDE * PLANE
CHEB = 6
GROUPS = 16
ORB = 32
PAIRS = 160
PARTS = ((0, 24), (96, 16))
BLOCK = 32
F32, BF16, I32 = jnp.float32, jnp.bfloat16, jnp.int32
MESH = pl.DeviceIdType.MESH

NN = (((1,), (0,)), ((), ()))
NT = (((1,), (1,)), ((), ()))
TN = (((0,), (0,)), ((), ()))


def operator_1d():
    weights = {0: -49.0 / 18.0, 1: 1.5, 2: -0.15, 3: 1.0 / 90.0}
    a = np.zeros((SIDE, SIDE))
    for i in range(SIDE):
        for j in range(SIDE):
            a[i, j] = -weights.get(abs(i - j), 0.0)
    return a


def eigen(a):
    a, n = a.copy(), a.shape[0]
    v = np.eye(n)
    for _ in range(10):
        for p in range(n - 1):
            for q in range(p + 1, n):
                if abs(a[p, q]) < 1e-18:
                    continue
                theta = (a[q, q] - a[p, p]) / (2.0 * a[p, q])
                t = (1.0 if theta >= 0 else -1.0) / (abs(theta) + math.sqrt(theta * theta + 1.0))
                c = 1.0 / math.sqrt(t * t + 1.0)
                s = t * c
                ap, aq = a[:, p].copy(), a[:, q].copy()
                a[:, p], a[:, q] = c * ap - s * aq, s * ap + c * aq
                ap, aq = a[p].copy(), a[q].copy()
                a[p], a[q] = c * ap - s * aq, s * ap + c * aq
                vp, vq = v[:, p].copy(), v[:, q].copy()
                v[:, p], v[:, q] = c * vp - s * vq, s * vp + c * vq
    return np.diag(a).copy(), v


def polynomial(lam):
    low, high = 3.0 * (math.pi / (SIDE + 1)) ** 2, 18.2
    mid, half = 0.5 * (high + low), 0.5 * (high - low)
    alpha, beta = 1.0 / mid, 0.0
    x, res, p = np.zeros_like(lam), np.ones_like(lam), np.zeros_like(lam)
    for k in range(1, CHEB + 1):
        if k > 1:
            beta = 0.5 * (half * alpha) ** 2 if k == 2 else (0.5 * half * alpha) ** 2
            alpha = 1.0 / (mid - beta / alpha)
        p = res + beta * p
        x = x + alpha * p
        res = res - alpha * lam * p
    return x


def halves(a):
    high = a.astype(BF16)
    low = (a - high.astype(np.float64)).astype(BF16)
    return np.stack([high, low])


def constants():
    lam, q = eigen(operator_1d())
    plane = halves(np.kron(q, q))
    lines = halves(np.stack([np.kron(q.T, np.eye(8)), np.kron(q, np.eye(8))]))
    total = lam[:, None, None] + lam[None, :, None] + lam[None, None, :]
    table = polynomial(total).reshape(SIDE, PLANE).astype(np.float32)
    return plane, lines, table


def iota(shape, dim):
    return lax.broadcasted_iota(I32, shape, dim)


def roll(x, n, axis):
    n %= x.shape[axis]
    return pltpu.roll(x, n, axis) if n else x


def lead(x, n):
    n %= x.shape[0]
    return jnp.concatenate([x[x.shape[0] - n :], x[: x.shape[0] - n]], 0) if n else x


def bit(o, b):
    return jnp.bitwise_and(jnp.right_shift(o, b), 1) > 0


def turn_rows(x, o2, o3, sign):
    third = jnp.bitwise_and(iota(x.shape, 1), SIDE - 1)
    b2 = jnp.broadcast_to(o2, x.shape)
    b3 = jnp.broadcast_to(o3, x.shape)
    for b in range(4):
        n = 1 << b
        x = jnp.where(bit(b2, b), roll(x, sign * SIDE * n, 1), x)
        inside = third >= n if sign > 0 else third < SIDE - n
        y = jnp.where(inside, roll(x, sign * n, 1), roll(x, sign * (n - SIDE), 1))
        x = jnp.where(bit(b3, b), y, x)
    return x


def turn_box(x, o, sign):
    o1, o2, o3 = (jnp.broadcast_to(v, x.shape) for v in o)
    lane = iota(x.shape, 2)
    third = jnp.bitwise_and(lane, SIDE - 1)
    for b in range(4):
        n = 1 << b
        x = jnp.where(bit(o1, b), lead(x, sign * n), x)
        if b < 2:
            y = roll(x, sign * SIDE * n, 2)
            kept = lane >= SIDE * n if sign > 0 else lane < 128 - SIDE * n
            y = jnp.where(kept, y, roll(y, sign, 1))
        else:
            y = roll(x, sign * n // 4, 1)
        x = jnp.where(bit(o2, b), y, x)
        inside = third >= n if sign > 0 else third < SIDE - n
        y = jnp.where(inside, roll(x, sign * n, 2), roll(x, sign * (n - SIDE), 2))
        x = jnp.where(bit(o3, b), y, x)
    return x


def turn_lead(x, o1, sign):
    o = jnp.broadcast_to(o1, x.shape[1:])[None]
    for b in range(4):
        x = jnp.where(bit(o, b), lead(x, sign << b if sign > 0 else -(1 << b)), x)
    return x


def split(x):
    high = x.astype(BF16)
    return high, (x - high.astype(F32)).astype(BF16)


def dot(a, b, dims=NN):
    return lax.dot_general(a, b, dims, preferred_element_type=F32)


def rotated(x, y, core, t):
    m = lax.rem(t * 5, 16)
    return (
        lax.rem(x + lax.div(m, 4), 4),
        lax.rem(y + lax.rem(m, 4), 4),
        lax.rem(core + lax.div(t, 16), 2),
    )


def device(x, y, z, c):
    return x * 4 + lax.div(z, 8) * 2 + c, y * 8 + lax.rem(z, 8)


def kernel(
    box_ref, offsets_ref, slots_ref, plane_ref, lines_ref, table_ref,
    field_ref, gram_ref,
    plane, lines, table, own, mid, pair_out, boxes_out, pair_in, near_in, far_in, cells,
    ohl, ohr, offs, lm, rm, dh, dl, eh, el, modes, in_a, in_b, out_a, out_b, back, pots,
    field, far_field, prev_field, tiles, gp, send6, fin, gram_out, gram_fin,
    const_sem, send1, recv1, send2, recv2, send3, recv3, send4, recv4, send5, recv5,
    send6s, recv6, send6g, recv6g,
):
    gi, si = lax.axis_index("grp"), lax.axis_index("slab")
    x, zh, core = lax.div(gi, 4), lax.rem(lax.div(gi, 2), 2), lax.rem(gi, 2)
    y, zl = lax.div(si, 8), lax.rem(si, 8)
    z = zh * 8 + zl
    q = x * 4 + y
    rho = q * 2 + core
    role = z
    nxt = lax.rem(role + 1, GROUPS)

    entry = pltpu.get_barrier_semaphore()

    @pl.loop(1, 32)
    def _(t):
        peer = rotated(x, y, core, t)
        pl.semaphore_signal(entry, 1, device_id=device(peer[0], peer[1], z, peer[2]), device_id_type=MESH)

    @pl.loop(1, 16)
    def _(t):
        for c in range(2):
            pl.semaphore_signal(entry, 1, device_id=device(x, y, lax.rem(z + t, 16), c), device_id_type=MESH)

    @pl.loop(0, 32)
    def _(t):
        px, py, pc = lax.div(t, 8), lax.rem(lax.div(t, 2), 4), lax.rem(t, 2)
        other = jnp.logical_or(gi != z, jnp.logical_or(px * 4 + py != q, pc != core))

        @pl.when(other)
        def _():
            pl.semaphore_signal(entry, 1, device_id=device(px, py, gi, pc), device_id_type=MESH)

    served = jnp.where(gi == z, 31, 32)
    consts = [
        pltpu.make_async_copy(plane_ref, plane, const_sem.at[0]),
        pltpu.make_async_copy(lines_ref, lines, const_sem.at[1]),
        pltpu.make_async_copy(table_ref, table, const_sem.at[2]),
    ]
    for c in consts:
        c.start()

    row = iota((72, 512), 0)
    local = lax.rem(row, ORB)
    ident = jnp.where(row < ORB, role, nxt) * ORB + lax.rem(local, 4) * 8 + lax.div(local, 4)
    ident = jnp.where(row < 2 * ORB, ident, gi * ORB + si)
    pick = (ident == iota((72, 512), 1)).astype(BF16)
    found = dot(pick, offsets_ref[...].astype(BF16), NT)
    own_o = [found[64:65, d : d + 1].astype(I32).reshape(1, 1, 1) for d in range(3)]

    box = turn_box(box_ref[...].astype(F32).reshape(256, 128).reshape(SIDE, 8, 128), own_o, 1)
    own[:, 0] = box.reshape(16, 16, 128).astype(BF16)
    ids = slots_ref[...]
    side = iota((8, 128), 1)
    slots = jnp.full((8, 128), -1, I32)
    for k in range(6):
        at = iota((8, 128), 0) == k
        for c in range(2):
            one = jnp.broadcast_to(ids[c : c + 1, k : k + 1], (8, 128))
            slots = jnp.where(jnp.logical_and(at, side == c), one, slots)
    member = lax.rem(slots, ORB)
    spot = lax.rem(member, 8) * 4 + lax.div(member, 8)
    spot = spot + jnp.where(lax.div(slots, ORB) == gi, 0, ORB)
    spot = jnp.where(slots >= 0, spot, -1).astype(F32)
    own[:, 1] = jnp.broadcast_to(jnp.concatenate([spot, spot], 0).astype(BF16)[None], (16, 16, 128))

    pltpu.make_async_copy(own.at[q], mid.at[q], recv1).start()
    pl.semaphore_wait(entry, 61 + served)

    @pl.loop(1, 16)
    def _(t):
        px, py, _ = rotated(x, y, core, t)
        pltpu.make_async_remote_copy(
            own.at[px * 4 + py], mid.at[q], send1, recv1, device(px, py, z, core), MESH
        ).start()

    pltpu.make_async_copy(mid, mid, recv1).wait()

    heap = mid[:, 0].astype(F32).reshape(4, 4, 2, 8, 128)
    lists = mid[:, 1].astype(F32)[:, :8].reshape(4, 4, 8, 128)
    row8, lane8 = iota((8, 128), 0), iota((8, 128), 1)
    for g in range(4):
        merged = jnp.where(lane8 < 2, lists[g, 0], 0.0)
        for j in range(1, 4):
            merged = merged + jnp.where(lax.div(lane8, 2) == j, roll(lists[g, j], 2 * j, 1), 0.0)
        spread = merged
        for t in range(1, 6):
            spread = spread + roll(merged, 8 * t, 1)
        spread = jnp.where(lax.div(lane8, 8) == row8, spread, 0.0)
        pair_out[g] = jnp.sum(spread, axis=0, keepdims=True)
        for c in range(2):
            part = heap[g, :, c].reshape(2, 16, 128).astype(BF16)
            boxes_out[g, c] = part
    sends2 = []
    for kind in range(3):
        for k in range(4):
            g = lax.rem(k + zl, 4)
            for c in range(2):
                target = lax.rem(g * 4 + zh * 2 + core + GROUPS - (1 if kind == 2 else 0), GROUPS)
                here = jnp.logical_and(target == z, core == c)
                out = pair_out.at[g] if kind == 0 else boxes_out.at[g, c]
                into = (pair_in, near_in, far_in)[kind].at[zl]
                remote = pltpu.make_async_remote_copy(
                    out, into, send2.at[kind, k, c], recv2.at[kind], device(x, y, target, c), MESH
                )
                local_copy = pltpu.make_async_copy(out, into, recv2.at[kind])
                pl.when(here)(local_copy.start)
                pl.when(jnp.logical_not(here))(remote.start)
                sends2.append((here, remote))
    pltpu.make_async_copy(own.at[pl.ds(0, 15)], own.at[pl.ds(0, 15)], send1).wait()
    pltpu.make_async_copy(pair_in, pair_in, recv2.at[0]).wait()

    lists = pair_in[...].reshape(8, 128)
    spots = [(8 * t + 2 * j) for t in range(6) for j in range(4)]
    left = jnp.concatenate([lists[:, a : a + 1] for a in spots], 0)
    right = jnp.concatenate([lists[:, a + 1 : a + 2] for a in spots], 0)
    live = left >= 0
    live_f = jnp.where(live, 1.0, 0.0)
    before = (iota((192, 192), 1) < iota((192, 192), 0)).astype(BF16)
    rank = dot(before, jnp.broadcast_to(live_f, (192, 128)).astype(BF16))[:, 0:1]
    rank = jnp.where(live, rank, -1.0)
    chosen = (jnp.broadcast_to(rank, (192, 256)) == iota((192, 256), 1).astype(F32)).astype(BF16)
    orbital = iota((192, 128), 1).astype(F32)
    pick_l = (jnp.broadcast_to(left, (192, 128)) == orbital).astype(BF16)
    pick_r = (jnp.broadcast_to(right, (192, 128)) == orbital).astype(BF16)
    one_l = dot(chosen, pick_l, TN)[:PAIRS]
    one_r = dot(chosen, pick_r, TN)[:PAIRS]
    ohl[...] = one_l
    ohr[...] = one_r
    o3 = jnp.concatenate([found[:64], jnp.zeros((64, found.shape[1]), F32)], 0)
    offs[...] = jnp.broadcast_to(dot(one_l.astype(BF16), o3.astype(BF16))[:, :3], (PAIRS, 3)).astype(I32)

    lane = iota((64, PLANE), 1)
    o = [jnp.broadcast_to(found[:64, d : d + 1], (64, PLANE)) for d in range(3)]
    code = jnp.where(rho.astype(F32) < o[0], 1.0, 0.0)
    code = code + jnp.where(lax.div(lane, SIDE).astype(F32) < o[1], 2.0, 0.0)
    code = code + jnp.where(jnp.bitwise_and(lane, SIDE - 1).astype(F32) < o[2], 4.0, 0.0)
    pltpu.make_async_copy(near_in, near_in, recv2.at[1]).wait()
    pltpu.make_async_copy(far_in, far_in, recv2.at[2]).wait()
    cells[0:256] = near_in[...].astype(F32).reshape(256, 128)
    cells[256:512] = far_in[...].astype(F32).reshape(256, 128)
    orbs = jnp.concatenate([cells[pl.ds(r, 64, stride=8), :] for r in range(8)], 1)
    both = jnp.concatenate([orbs, code], 1).astype(BF16)
    both = jnp.concatenate([both, jnp.zeros((64, 2 * PLANE), BF16)], 0)

    for b in range(PAIRS // BLOCK):
        rows = slice(b * BLOCK, (b + 1) * BLOCK)
        lv = dot(ohl[rows].astype(BF16), both)
        rv = dot(ohr[rows].astype(BF16), both)
        same = lv[:, PLANE:] == rv[:, PLANE:]
        lmv = jnp.where(same, lv[:, :PLANE], 0.0)
        rmv = jnp.where(same, rv[:, :PLANE], 0.0)
        lm[rows] = lmv
        rm[rows] = rmv
        dens = turn_rows(lmv * rmv, offs[rows, 1:2], offs[rows, 2:3], -1)
        dh[rows], dl[rows] = split(dens)

    for c in consts:
        c.wait()

    def part_of(ref, r, part):
        base, size = PARTS[part]
        return ref.at[
            pl.ds(pl.multiple_of(base + lax.div(r, 8) * size, 8), size),
            pl.ds(pl.multiple_of(lax.rem(r, 8) * 128, 128), 128),
        ]

    lines_in, lines_out = (in_a, in_b), (out_a, out_b)
    for part, (base, size) in enumerate(PARTS):
        rows = slice(base, base + 4 * size)
        landing = lines_in[part].at[rho]
        for dy in (2, 1, 3, 0):
            py = lax.rem(y + dy, 4)
            cols = pl.ds(pl.multiple_of(py * 256, 256), 256)
            wh, wl = plane[0, :, cols], plane[1, :, cols]
            modes[rows, cols] = dot(dh[rows], wh) + dot(dl[rows], wh) + dot(dh[rows], wl)
            for dx in (2, 1, 3, 0):
                for dc in (1, 0):
                    px, pc = lax.rem(x + dx, 4), lax.rem(core + dc, 2)
                    out = part_of(modes, px * 8 + py * 2 + pc, part)
                    if (dx, dy, dc) == (0, 0, 0):
                        pltpu.make_async_copy(out, landing, recv3.at[part]).start()
                    else:
                        pltpu.make_async_remote_copy(
                            out, landing, send3.at[part], recv3.at[part], device(px, py, z, pc), MESH
                        ).start()

    u, v = lax.div(rho, 8), lax.rem(rho, 8)
    scale = table[:, pl.ds(pl.multiple_of(v * 128, 128), 128)]
    scale = jnp.broadcast_to(scale[:, None, :], (SIDE, 8, 128)).reshape(256, 128)
    for part, (base, size) in enumerate(PARTS):
        source, result = lines_in[part], lines_out[part]
        pltpu.make_async_copy(source, source, recv3.at[part]).wait()
        for j in range(size // 8):
            rows = slice(8 * j, 8 * j + 8)
            o1 = offs[pl.ds(pl.multiple_of(base + u * size + 8 * j, 8), 8), 0:1]
            s = turn_lead(source[:, rows, :], o1, -1).reshape(256, 128)
            for way in range(2):
                sh, sl = split(s)
                s = dot(lines[0, way], sh) + dot(lines[0, way], sl) + dot(lines[1, way], sh)
                if way == 0:
                    s = s * scale
            result[:, rows, :] = turn_lead(s.reshape(SIDE, 8, 128), o1, 1)

        landing = part_of(back, rho, part)
        pltpu.make_async_copy(result.at[rho], landing, recv4.at[part]).start()

        @pl.loop(1, 32)
        def _(t):
            px, py, pc = rotated(x, y, core, t)
            r = px * 8 + py * 2 + pc
            pltpu.make_async_remote_copy(
                result.at[r], landing, send4.at[part], recv4.at[part], device(px, py, z, pc), MESH
            ).start()

    for part, (base, size) in enumerate(PARTS):
        rows = slice(base, base + 4 * size)
        arrived = back.at[pl.ds(base, 4 * size)]
        pltpu.make_async_copy(arrived, arrived, recv4.at[part]).wait()
        dh[rows], dl[rows] = split(back[rows])
        for n in range(4):
            cols = slice(n * 256, (n + 1) * 256)
            wh, wl = plane[0, cols, :], plane[1, cols, :]
            pots[rows, cols] = dot(dh[rows], wh, NT) + dot(dl[rows], wh, NT) + dot(dh[rows], wl, NT)
        for b in range(4 * size // BLOCK):
            rows = slice(base + b * BLOCK, base + (b + 1) * BLOCK)
            pot = turn_rows(pots[rows], offs[rows, 1:2], offs[rows, 2:3], 1)
            dh[rows], dl[rows] = split(pot * lm[rows])
            eh[rows], el[rows] = split(pot * rm[rows])
    pick_f = ohr[:, ORB : 2 * ORB].astype(BF16)
    far_field[...] = dot(pick_f, dh[...], TN) + dot(pick_f, dl[...], TN)

    far_copies = []
    for t in range(4):
        k = lax.rem(lax.div(lax.rem(zl + 1, 8), 2) + t, 4)
        rows = pl.ds(pl.multiple_of(8 * k, 8), 8)
        far_copies.append(
            pltpu.make_async_remote_copy(
                far_field.at[rows], prev_field.at[rows], send5.at[t], recv5.at[k], device(x, y, nxt, core), MESH
            )
        )
        far_copies[-1].start()
    pick_f = ohr[:, 0:ORB].astype(BF16)
    total = dot(pick_f, dh[...], TN) + dot(pick_f, dl[...], TN)
    pick_f = ohl[:, 0:ORB].astype(BF16)
    field[...] = total + dot(pick_f, eh[...], TN) + dot(pick_f, el[...], TN)
    framed = jnp.where(code[:ORB] == code[0:1], orbs[:ORB], 0.0)
    perm_row = iota((128, ORB), 0)
    perm = (lax.rem(perm_row, 8) * 4 + lax.div(perm_row, 8) == iota((128, ORB), 1)) & (perm_row < ORB)
    framed = dot(perm.astype(BF16), framed.astype(BF16)).astype(BF16)
    home_x, home_zh, home_c = lax.div(role, 4), lax.rem(lax.div(role, 2), 2), lax.rem(role, 2)
    home_g = home_x * 4 + home_zh * 2 + home_c

    def send_home(k, j, out, into, send, recv):
        here = jnp.logical_and(home_g == gi, j * 8 + k == si)
        remote = pltpu.make_async_remote_copy(out, into, send, recv, (home_g, j * 8 + k), MESH)
        pl.when(here)(pltpu.make_async_copy(out, into, recv).start)
        pl.when(jnp.logical_not(here))(remote.start)

    for t in range(4):
        pair = lax.rem(lax.div(zl, 2) + t, 4)
        rows = pl.ds(pl.multiple_of(8 * pair, 8), 8)
        arrived = prev_field.at[rows]
        pltpu.make_async_copy(arrived, arrived, recv5.at[pair]).wait()
        summed = field[rows] + prev_field[rows]
        field[rows] = summed
        for r in range(8):
            tiles[pl.ds(r, 8, stride=8), :] = summed[:, r * 128 : (r + 1) * 128]
        send6[pl.ds(pl.multiple_of(8 * pair, 8), 8)] = tiles[...].reshape(8, 8, 128)

        @pl.loop(0, 8)
        def _(i):
            k, j = 2 * pair + lax.rem(i, 2), lax.rem(y + lax.div(i, 2), 4)
            send_home(k, j, send6.at[4 * k + j], fin.at[rho], send6s, recv6)

    framed_field = jnp.where(code[:ORB] == code[0:1], field[...], 0.0).astype(BF16)
    gp[...] = dot(framed_field, framed, NT)
    for k in range(ORB):
        gram_out[k] = gp[k : k + 1]

    @pl.loop(0, ORB)
    def _(i):
        k, j = lax.rem(zl + lax.rem(i, 8), 8), lax.rem(y + lax.div(i, 8), 4)
        send_home(k, j, gram_out.at[4 * k + j], gram_fin.at[rho], send6g, recv6g)

    pltpu.make_async_copy(fin, fin, recv6).wait()
    field_ref[...] = turn_box(fin[...], own_o, -1).reshape(256, 128)
    pltpu.make_async_copy(gram_fin, gram_fin, recv6g).wait()
    gram_ref[...] = jnp.sum(gram_fin[...], axis=0) * (1.0 / math.sqrt(CELLS))

    rest = pl.ds(0, 31)
    for sent, sem in ((fin, send6s), (gram_fin, send6g)):
        pltpu.make_async_copy(sent.at[rest], sent.at[rest], sem).wait()
        one = pltpu.make_async_copy(sent.at[0], sent.at[0], sem)
        pl.when(home_g != gi)(one.wait)

    for here, remote in sends2:
        pl.when(jnp.logical_not(here))(remote.wait_send)
    for part in range(2):
        sent = lines_in[part].at[pl.ds(0, 31)]
        pltpu.make_async_copy(sent, sent, send3.at[part]).wait()
        pltpu.make_async_copy(sent, sent, send4.at[part]).wait()
    for far_copy in far_copies:
        far_copy.wait_send()


def on_device(orbitals, offsets, slot_pairs):
    plane_c, lines_c, table_c = constants()
    vmem = pl.BlockSpec(memory_space=pltpu.VMEM)
    hbm = pl.BlockSpec(memory_space=pltpu.HBM)
    dma = pltpu.SemaphoreType.DMA
    scratch = [
        pltpu.VMEM((2, PLANE, PLANE), BF16),
        pltpu.VMEM((2, 2, 256, 256), BF16),
        pltpu.VMEM((SIDE, PLANE), F32),
        pltpu.VMEM((16, 2, 16, 128), BF16),
        pltpu.VMEM((16, 2, 16, 128), BF16),
        pltpu.VMEM((4, 1, 128), F32),
        pltpu.VMEM((4, 2, 2, 16, 128), BF16),
        pltpu.VMEM((8, 1, 128), F32),
        pltpu.VMEM((8, 2, 16, 128), BF16),
        pltpu.VMEM((8, 2, 16, 128), BF16),
        pltpu.VMEM((512, 128), F32),
        pltpu.VMEM((PAIRS, 128), F32),
        pltpu.VMEM((PAIRS, 128), F32),
        pltpu.VMEM((PAIRS, 3), I32),
        pltpu.VMEM((PAIRS, PLANE), F32),
        pltpu.VMEM((PAIRS, PLANE), F32),
        pltpu.VMEM((PAIRS, PLANE), BF16),
        pltpu.VMEM((PAIRS, PLANE), BF16),
        pltpu.VMEM((PAIRS, PLANE), BF16),
        pltpu.VMEM((PAIRS, PLANE), BF16),
        pltpu.VMEM((PAIRS, PLANE), F32),
        pltpu.VMEM((32, PARTS[0][1], 128), F32),
        pltpu.VMEM((32, PARTS[1][1], 128), F32),
        pltpu.VMEM((32, PARTS[0][1], 128), F32),
        pltpu.VMEM((32, PARTS[1][1], 128), F32),
        pltpu.VMEM((PAIRS, PLANE), F32),
        pltpu.VMEM((PAIRS, PLANE), F32),
        pltpu.VMEM((ORB, PLANE), F32),
        pltpu.VMEM((ORB, PLANE), F32),
        pltpu.VMEM((ORB, PLANE), F32),
        pltpu.VMEM((64, 128), F32),
        pltpu.VMEM((ORB, 128), F32),
        pltpu.VMEM((ORB, 8, 128), F32),
        pltpu.VMEM((32, 8, 128), F32),
        pltpu.VMEM((ORB, 1, 128), F32),
        pltpu.VMEM((32, 1, 128), F32),
        dma((3,)),
        dma, dma,
        dma((3, 4, 2)), dma((3,)),
        dma((2,)), dma((2,)),
        dma((2,)), dma((2,)),
        dma((4,)), dma((4,)),
        dma, dma, dma, dma,
    ]
    field, gram = pl.pallas_call(
        kernel,
        out_shape=(jax.ShapeDtypeStruct((256, 128), F32), jax.ShapeDtypeStruct((1, 128), F32)),
        in_specs=[vmem, vmem, vmem, hbm, hbm, hbm],
        out_specs=(vmem, vmem),
        scratch_shapes=scratch,
        compiler_params=pltpu.CompilerParams(has_side_effects=True, collective_id=1, vmem_limit_bytes=63 * 2**20),
    )(
        orbitals,
        offsets.T,
        slot_pairs.T,
        jnp.asarray(plane_c),
        jnp.asarray(lines_c),
        jnp.asarray(table_c),
    )
    return field.reshape(1, CELLS), gram[0, :ORB].reshape(1, ORB, 1)


def solution(mesh):
    return jax.shard_map(
        on_device,
        mesh=mesh,
        in_specs=(P(("grp", "slab"), None), P(), P(("grp", "slab"), None)),
        out_specs=(P(("grp", "slab"), None), P("grp", None, "slab")),
        check_vma=False,
    )
```

```python
import math

import jax
import jax.numpy as jnp
import numpy as np
from jax import lax
from jax.experimental import pallas as pl
from jax.experimental.pallas import tpu as pltpu
from jax.sharding import PartitionSpec as P

SIDE = 32
PLANE = SIDE * SIDE
CELLS = SIDE * PLANE
CHEB = 6
GROUPS = 16
ORB = 32
PAIRS = 160
SIZES = (8, 16, 16)
PARTS = tuple((4 * sum(SIZES[:i]), n) for i, n in enumerate(SIZES))
BLOCK = 32
F32, BF16, I32 = jnp.float32, jnp.bfloat16, jnp.int32
MESH = pl.DeviceIdType.MESH

NN = (((1,), (0,)), ((), ()))
NT = (((1,), (1,)), ((), ()))
TN = (((0,), (0,)), ((), ()))


def operator_1d():
    weights = {0: -49.0 / 18.0, 1: 1.5, 2: -0.15, 3: 1.0 / 90.0}
    a = np.zeros((SIDE, SIDE))
    for i in range(SIDE):
        for j in range(SIDE):
            a[i, j] = -weights.get(abs(i - j), 0.0)
    return a


def eigen(a):
    a, n = a.copy(), a.shape[0]
    v = np.eye(n)
    for _ in range(10):
        for p in range(n - 1):
            for q in range(p + 1, n):
                if abs(a[p, q]) < 1e-18:
                    continue
                theta = (a[q, q] - a[p, p]) / (2.0 * a[p, q])
                t = (1.0 if theta >= 0 else -1.0) / (abs(theta) + math.sqrt(theta * theta + 1.0))
                c = 1.0 / math.sqrt(t * t + 1.0)
                s = t * c
                ap, aq = a[:, p].copy(), a[:, q].copy()
                a[:, p], a[:, q] = c * ap - s * aq, s * ap + c * aq
                ap, aq = a[p].copy(), a[q].copy()
                a[p], a[q] = c * ap - s * aq, s * ap + c * aq
                vp, vq = v[:, p].copy(), v[:, q].copy()
                v[:, p], v[:, q] = c * vp - s * vq, s * vp + c * vq
    return np.diag(a).copy(), v


def polynomial(lam):
    low, high = 3.0 * (math.pi / (SIDE + 1)) ** 2, 18.2
    mid, half = 0.5 * (high + low), 0.5 * (high - low)
    alpha, beta = 1.0 / mid, 0.0
    x, res, p = np.zeros_like(lam), np.ones_like(lam), np.zeros_like(lam)
    for k in range(1, CHEB + 1):
        if k > 1:
            beta = 0.5 * (half * alpha) ** 2 if k == 2 else (0.5 * half * alpha) ** 2
            alpha = 1.0 / (mid - beta / alpha)
        p = res + beta * p
        x = x + alpha * p
        res = res - alpha * lam * p
    return x


def halves(a):
    high = a.astype(BF16)
    low = (a - high.astype(np.float64)).astype(BF16)
    return np.stack([high, low])


def constants():
    lam, q = eigen(operator_1d())
    plane = halves(np.kron(q, q))
    lines = np.stack([halves(np.kron(q.T, np.eye(8))), halves(np.kron(q, np.eye(8)))])
    total = lam[:, None, None] + lam[None, :, None] + lam[None, None, :]
    table = polynomial(total).reshape(SIDE, PLANE).astype(np.float32)
    return plane, lines, table


def iota(shape, dim):
    return lax.broadcasted_iota(I32, shape, dim)


def roll(x, n, axis):
    n %= x.shape[axis]
    return pltpu.roll(x, n, axis) if n else x


def lead(x, n):
    n %= x.shape[0]
    return jnp.concatenate([x[x.shape[0] - n :], x[: x.shape[0] - n]], 0) if n else x


def bit(o, b):
    return jnp.bitwise_and(jnp.right_shift(o, b), 1) > 0


def turn_rows(x, o2, o3, sign):
    third = jnp.bitwise_and(iota(x.shape, 1), SIDE - 1)
    b2 = jnp.broadcast_to(o2, x.shape)
    b3 = jnp.broadcast_to(o3, x.shape)
    for b in range(4):
        n = 1 << b
        x = jnp.where(bit(b2, b), roll(x, sign * SIDE * n, 1), x)
        inside = third >= n if sign > 0 else third < SIDE - n
        y = jnp.where(inside, roll(x, sign * n, 1), roll(x, sign * (n - SIDE), 1))
        x = jnp.where(bit(b3, b), y, x)
    return x


def turn_box(x, o, sign):
    o1, o2, o3 = (jnp.broadcast_to(v, x.shape) for v in o)
    lane = iota(x.shape, 2)
    third = jnp.bitwise_and(lane, SIDE - 1)
    for b in range(4):
        n = 1 << b
        x = jnp.where(bit(o1, b), lead(x, sign * n), x)
        if b < 2:
            y = roll(x, sign * SIDE * n, 2)
            kept = lane >= SIDE * n if sign > 0 else lane < 128 - SIDE * n
            y = jnp.where(kept, y, roll(y, sign, 1))
        else:
            y = roll(x, sign * n // 4, 1)
        x = jnp.where(bit(o2, b), y, x)
        inside = third >= n if sign > 0 else third < SIDE - n
        y = jnp.where(inside, roll(x, sign * n, 2), roll(x, sign * (n - SIDE), 2))
        x = jnp.where(bit(o3, b), y, x)
    return x


def turn_lead(x, o1, sign):
    o = jnp.broadcast_to(o1, x.shape[1:])[None]
    for b in range(4):
        x = jnp.where(bit(o, b), lead(x, sign << b if sign > 0 else -(1 << b)), x)
    return x


def split(x):
    high = x.astype(BF16)
    return high, (x - high.astype(F32)).astype(BF16)


def dot(a, b, dims=NN):
    return lax.dot_general(a, b, dims, preferred_element_type=F32)


def three(high, low, matrix_high, matrix_low, dims=NN):
    n = high.shape[0]
    both = dot(jnp.concatenate([high, low], 0), matrix_high, dims)
    return both[:n] + both[n:] + dot(high, matrix_low, dims)


def rotated(x, y, core, t):
    m = lax.rem(t * 5, 16)
    return (
        lax.rem(x + lax.div(m, 4), 4),
        lax.rem(y + lax.rem(m, 4), 4),
        lax.rem(core + lax.div(t, 16), 2),
    )


def device(x, y, z, c):
    return x * 4 + lax.div(z, 8) * 2 + c, y * 8 + lax.rem(z, 8)


def kernel(
    box_ref, offsets_ref, slots_ref, plane_ref, lines_ref, table_ref,
    field_ref, gram_ref,
    plane, lines, table, own, mid, pair_out, boxes_out, pair_in, near_in, far_in, cells,
    ohl, ohr, offs, lm, rm, dh, dl, eh, el, modes, lines_in, lines_out, back, pots,
    field, far_field, prev_field, tiles, gp, send6, fin, gram_out, gram_fin,
    const_sem, send1, recv1, send2, recv2, send3, recv3, send4, recv4, send5, recv5,
    send6s, recv6, send6g, recv6g,
):
    gi, si = lax.axis_index("grp"), lax.axis_index("slab")
    x, zh, core = lax.div(gi, 4), lax.rem(lax.div(gi, 2), 2), lax.rem(gi, 2)
    y, zl = lax.div(si, 8), lax.rem(si, 8)
    z = zh * 8 + zl
    q = x * 4 + y
    rho = q * 2 + core
    role = z
    nxt = lax.rem(role + 1, GROUPS)

    entry = pltpu.get_barrier_semaphore()

    @pl.loop(1, 32)
    def _(t):
        peer = rotated(x, y, core, t)
        pl.semaphore_signal(entry, 1, device_id=device(peer[0], peer[1], z, peer[2]), device_id_type=MESH)

    @pl.loop(1, 16)
    def _(t):
        for c in range(2):
            pl.semaphore_signal(entry, 1, device_id=device(x, y, lax.rem(z + t, 16), c), device_id_type=MESH)

    @pl.loop(0, 32)
    def _(t):
        px, py, pc = lax.div(t, 8), lax.rem(lax.div(t, 2), 4), lax.rem(t, 2)
        other = jnp.logical_or(gi != z, jnp.logical_or(px * 4 + py != q, pc != core))

        @pl.when(other)
        def _():
            pl.semaphore_signal(entry, 1, device_id=device(px, py, gi, pc), device_id_type=MESH)

    served = jnp.where(gi == z, 31, 32)
    consts = [
        pltpu.make_async_copy(plane_ref, plane, const_sem.at[0]),
        pltpu.make_async_copy(lines_ref, lines, const_sem.at[1]),
        pltpu.make_async_copy(table_ref, table, const_sem.at[2]),
    ]
    for c in consts:
        c.start()

    row = iota((72, 512), 0)
    local = lax.rem(row, ORB)
    ident = jnp.where(row < ORB, role, nxt) * ORB + lax.rem(local, 4) * 8 + lax.div(local, 4)
    ident = jnp.where(row < 2 * ORB, ident, gi * ORB + si)
    pick = (ident == iota((72, 512), 1)).astype(BF16)
    found = dot(pick, offsets_ref[...].astype(BF16), NT)
    own_o = [found[64:65, d : d + 1].astype(I32).reshape(1, 1, 1) for d in range(3)]

    box = turn_box(box_ref[...].astype(F32).reshape(256, 128).reshape(SIDE, 8, 128), own_o, 1)
    own[:, 0] = box.reshape(16, 16, 128).astype(BF16)
    ids = slots_ref[...]
    side = iota((8, 128), 1)
    slots = jnp.full((8, 128), -1, I32)
    for k in range(6):
        at = iota((8, 128), 0) == k
        for c in range(2):
            one = jnp.broadcast_to(ids[c : c + 1, k : k + 1], (8, 128))
            slots = jnp.where(jnp.logical_and(at, side == c), one, slots)
    member = lax.rem(slots, ORB)
    spot = lax.rem(member, 8) * 4 + lax.div(member, 8)
    spot = spot + jnp.where(lax.div(slots, ORB) == gi, 0, ORB)
    spot = jnp.where(slots >= 0, spot, -1).astype(F32)
    own[:, 1] = jnp.broadcast_to(jnp.concatenate([spot, spot], 0).astype(BF16)[None], (16, 16, 128))

    pltpu.make_async_copy(own.at[q], mid.at[q], recv1).start()
    pl.semaphore_wait(entry, 61 + served)

    @pl.loop(1, 16)
    def _(t):
        px, py, _ = rotated(x, y, core, t)
        pltpu.make_async_remote_copy(
            own.at[px * 4 + py], mid.at[q], send1, recv1, device(px, py, z, core), MESH
        ).start()

    pltpu.make_async_copy(mid, mid, recv1).wait()

    heap = mid[:, 0].astype(F32).reshape(4, 4, 2, 8, 128)
    lists = mid[:, 1].astype(F32)[:, :8].reshape(4, 4, 8, 128)
    row8, lane8 = iota((8, 128), 0), iota((8, 128), 1)
    for g in range(4):
        merged = jnp.where(lane8 < 2, lists[g, 0], 0.0)
        for j in range(1, 4):
            merged = merged + jnp.where(lax.div(lane8, 2) == j, roll(lists[g, j], 2 * j, 1), 0.0)
        spread = merged
        for t in range(1, 6):
            spread = spread + roll(merged, 8 * t, 1)
        spread = jnp.where(lax.div(lane8, 8) == row8, spread, 0.0)
        pair_out[g] = jnp.sum(spread, axis=0, keepdims=True)
        for c in range(2):
            part = heap[g, :, c].reshape(2, 16, 128).astype(BF16)
            boxes_out[g, c] = part
    sends2 = []
    for kind in range(3):
        for k in range(4):
            g = lax.rem(k + zl, 4)
            for c in range(2):
                target = lax.rem(g * 4 + zh * 2 + core + GROUPS - (1 if kind == 2 else 0), GROUPS)
                here = jnp.logical_and(target == z, core == c)
                out = pair_out.at[g] if kind == 0 else boxes_out.at[g, c]
                into = (pair_in, near_in, far_in)[kind].at[zl]
                remote = pltpu.make_async_remote_copy(
                    out, into, send2.at[kind, k, c], recv2.at[kind], device(x, y, target, c), MESH
                )
                local_copy = pltpu.make_async_copy(out, into, recv2.at[kind])
                pl.when(here)(local_copy.start)
                pl.when(jnp.logical_not(here))(remote.start)
                sends2.append((here, remote))
    pltpu.make_async_copy(own.at[pl.ds(0, 15)], own.at[pl.ds(0, 15)], send1).wait()
    pltpu.make_async_copy(pair_in, pair_in, recv2.at[0]).wait()

    lists = pair_in[...].reshape(8, 128)
    spots = [(8 * t + 2 * j) for t in range(6) for j in range(4)]
    left = jnp.concatenate([lists[:, a : a + 1] for a in spots], 0)
    right = jnp.concatenate([lists[:, a + 1 : a + 2] for a in spots], 0)
    live = left >= 0
    live_f = jnp.where(live, 1.0, 0.0)
    before = (iota((192, 192), 1) < iota((192, 192), 0)).astype(BF16)
    rank = dot(before, jnp.broadcast_to(live_f, (192, 128)).astype(BF16))[:, 0:1]
    rank = jnp.where(live, rank, -1.0)
    chosen = (jnp.broadcast_to(rank, (192, 256)) == iota((192, 256), 1).astype(F32)).astype(BF16)
    orbital = iota((192, 128), 1).astype(F32)
    pick_l = (jnp.broadcast_to(left, (192, 128)) == orbital).astype(BF16)
    pick_r = (jnp.broadcast_to(right, (192, 128)) == orbital).astype(BF16)
    one_l = dot(chosen, pick_l, TN)[:PAIRS]
    one_r = dot(chosen, pick_r, TN)[:PAIRS]
    ohl[...] = one_l
    ohr[...] = one_r
    o3 = jnp.concatenate([found[:64], jnp.zeros((64, found.shape[1]), F32)], 0)
    offs[...] = jnp.broadcast_to(dot(one_l.astype(BF16), o3.astype(BF16))[:, :3], (PAIRS, 3)).astype(I32)

    lane = iota((64, PLANE), 1)
    o = [jnp.broadcast_to(found[:64, d : d + 1], (64, PLANE)) for d in range(3)]
    code = jnp.where(rho.astype(F32) < o[0], 1.0, 0.0)
    code = code + jnp.where(lax.div(lane, SIDE).astype(F32) < o[1], 2.0, 0.0)
    code = code + jnp.where(jnp.bitwise_and(lane, SIDE - 1).astype(F32) < o[2], 4.0, 0.0)
    pltpu.make_async_copy(near_in, near_in, recv2.at[1]).wait()
    pltpu.make_async_copy(far_in, far_in, recv2.at[2]).wait()
    cells[0:256] = near_in[...].astype(F32).reshape(256, 128)
    cells[256:512] = far_in[...].astype(F32).reshape(256, 128)
    orbs = jnp.concatenate([cells[pl.ds(r, 64, stride=8), :] for r in range(8)], 1)
    both = jnp.concatenate([orbs, code], 1).astype(BF16)
    both = jnp.concatenate([both, jnp.zeros((64, 2 * PLANE), BF16)], 0)

    for b in range(PAIRS // BLOCK):
        rows = slice(b * BLOCK, (b + 1) * BLOCK)
        lv = dot(ohl[rows].astype(BF16), both)
        rv = dot(ohr[rows].astype(BF16), both)
        same = lv[:, PLANE:] == rv[:, PLANE:]
        lmv = jnp.where(same, lv[:, :PLANE], 0.0)
        rmv = jnp.where(same, rv[:, :PLANE], 0.0)
        lm[rows] = lmv
        rm[rows] = rmv
        dens = turn_rows(lmv * rmv, offs[rows, 1:2], offs[rows, 2:3], -1)
        dh[rows], dl[rows] = split(dens)

    for c in consts:
        c.wait()

    def part_of(ref, r, part):
        base, size = PARTS[part]
        return ref.at[
            pl.ds(pl.multiple_of(base + lax.div(r, 8) * size, 8), size),
            pl.ds(pl.multiple_of(lax.rem(r, 8) * 128, 128), 128),
        ]

    def piece(ref, part, at=slice(None)):
        base, size = PARTS[part]
        return ref.at[at, base // 4 : base // 4 + size]

    for part, (base, size) in enumerate(PARTS):
        rows = slice(base, base + 4 * size)
        landing = piece(lines_in, part, rho)
        for dy in (2, 1, 3, 0):
            py = lax.rem(y + dy, 4)
            cols = pl.ds(pl.multiple_of(py * 256, 256), 256)
            wh, wl = plane[0, :, cols], plane[1, :, cols]
            modes[rows, cols] = three(dh[rows], dl[rows], wh, wl)
            for dx in (2, 1, 3, 0):
                for dc in (1, 0):
                    px, pc = lax.rem(x + dx, 4), lax.rem(core + dc, 2)
                    out = part_of(modes, px * 8 + py * 2 + pc, part)
                    if (dx, dy, dc) == (0, 0, 0):
                        pltpu.make_async_copy(out, landing, recv3.at[part]).start()
                    else:
                        pltpu.make_async_remote_copy(
                            out, landing, send3.at[part], recv3.at[part], device(px, py, z, pc), MESH
                        ).start()

    u, v = lax.div(rho, 8), lax.rem(rho, 8)
    scale = table[:, pl.ds(pl.multiple_of(v * 128, 128), 128)]
    scale = jnp.broadcast_to(scale[:, None, :], (SIDE, 8, 128)).reshape(256, 128)
    for part, (base, size) in enumerate(PARTS):
        pltpu.make_async_copy(piece(lines_in, part), piece(lines_in, part), recv3.at[part]).wait()
        for j in range(size // 8):
            rows = slice(base // 4 + 8 * j, base // 4 + 8 * j + 8)
            o1 = offs[pl.ds(pl.multiple_of(base + u * size + 8 * j, 8), 8), 0:1]
            s = turn_lead(lines_in[:, rows, :], o1, -1).reshape(256, 128)
            for way in range(2):
                sh, sl = split(s)
                both = dot(lines[way].reshape(512, 256), sh)
                s = both[:256] + both[256:] + dot(lines[way, 0], sl)
                if way == 0:
                    s = s * scale
            lines_out[:, rows, :] = turn_lead(s.reshape(SIDE, 8, 128), o1, 1)

        landing = part_of(back, rho, part)
        pltpu.make_async_copy(piece(lines_out, part, rho), landing, recv4.at[part]).start()

        @pl.loop(1, 32)
        def _(t):
            px, py, pc = rotated(x, y, core, t)
            r = px * 8 + py * 2 + pc
            pltpu.make_async_remote_copy(
                piece(lines_out, part, r), landing, send4.at[part], recv4.at[part], device(px, py, z, pc), MESH
            ).start()

    for part, (base, size) in enumerate(PARTS):
        rows = slice(base, base + 4 * size)
        arrived = back.at[pl.ds(base, 4 * size)]
        pltpu.make_async_copy(arrived, arrived, recv4.at[part]).wait()
        dh[rows], dl[rows] = split(back[rows])
        for n in range(4):
            cols = slice(n * 256, (n + 1) * 256)
            wh, wl = plane[0, cols, :], plane[1, cols, :]
            pots[rows, cols] = three(dh[rows], dl[rows], wh, wl, NT)
        for b in range(4 * size // BLOCK):
            rows = slice(base + b * BLOCK, base + (b + 1) * BLOCK)
            pot = turn_rows(pots[rows], offs[rows, 1:2], offs[rows, 2:3], 1)
            dh[rows], dl[rows] = split(pot * lm[rows])
            eh[rows], el[rows] = split(pot * rm[rows])
    pick_f = ohr[:, ORB : 2 * ORB].astype(BF16)
    far_field[...] = dot(pick_f, dh[...], TN) + dot(pick_f, dl[...], TN)

    far_copies = []
    for t in range(4):
        k = lax.rem(lax.div(lax.rem(zl + 1, 8), 2) + t, 4)
        rows = pl.ds(pl.multiple_of(8 * k, 8), 8)
        far_copies.append(
            pltpu.make_async_remote_copy(
                far_field.at[rows], prev_field.at[rows], send5.at[t], recv5.at[k], device(x, y, nxt, core), MESH
            )
        )
        far_copies[-1].start()
    pick_f = ohr[:, 0:ORB].astype(BF16)
    total = dot(pick_f, dh[...], TN) + dot(pick_f, dl[...], TN)
    pick_f = ohl[:, 0:ORB].astype(BF16)
    field[...] = total + dot(pick_f, eh[...], TN) + dot(pick_f, el[...], TN)
    framed = jnp.where(code[:ORB] == code[0:1], orbs[:ORB], 0.0)
    perm_row = iota((128, ORB), 0)
    perm = (lax.rem(perm_row, 8) * 4 + lax.div(perm_row, 8) == iota((128, ORB), 1)) & (perm_row < ORB)
    framed = dot(perm.astype(BF16), framed.astype(BF16)).astype(BF16)
    home_x, home_zh, home_c = lax.div(role, 4), lax.rem(lax.div(role, 2), 2), lax.rem(role, 2)
    home_g = home_x * 4 + home_zh * 2 + home_c

    def send_home(k, j, out, into, send, recv):
        here = jnp.logical_and(home_g == gi, j * 8 + k == si)
        remote = pltpu.make_async_remote_copy(out, into, send, recv, (home_g, j * 8 + k), MESH)
        pl.when(here)(pltpu.make_async_copy(out, into, recv).start)
        pl.when(jnp.logical_not(here))(remote.start)

    for t in range(4):
        pair = lax.rem(lax.div(zl, 2) + t, 4)
        rows = pl.ds(pl.multiple_of(8 * pair, 8), 8)
        arrived = prev_field.at[rows]
        pltpu.make_async_copy(arrived, arrived, recv5.at[pair]).wait()
        summed = field[rows] + prev_field[rows]
        field[rows] = summed
        for r in range(8):
            tiles[pl.ds(r, 8, stride=8), :] = summed[:, r * 128 : (r + 1) * 128]
        send6[pl.ds(pl.multiple_of(8 * pair, 8), 8)] = tiles[...].reshape(8, 8, 128)

        @pl.loop(0, 8)
        def _(i):
            k, j = 2 * pair + lax.rem(i, 2), lax.rem(y + lax.div(i, 2), 4)
            send_home(k, j, send6.at[4 * k + j], fin.at[rho], send6s, recv6)

    framed_field = jnp.where(code[:ORB] == code[0:1], field[...], 0.0).astype(BF16)
    gp[...] = dot(framed_field, framed, NT)
    for k in range(ORB):
        gram_out[k] = gp[k : k + 1]

    @pl.loop(0, ORB)
    def _(i):
        k, j = lax.rem(zl + lax.rem(i, 8), 8), lax.rem(y + lax.div(i, 8), 4)
        send_home(k, j, gram_out.at[4 * k + j], gram_fin.at[rho], send6g, recv6g)

    pltpu.make_async_copy(fin, fin, recv6).wait()
    field_ref[...] = turn_box(fin[...], own_o, -1).reshape(256, 128)
    pltpu.make_async_copy(gram_fin, gram_fin, recv6g).wait()
    gram_ref[...] = jnp.sum(gram_fin[...], axis=0) * (1.0 / math.sqrt(CELLS))

    rest = pl.ds(0, 31)
    for sent, sem in ((fin, send6s), (gram_fin, send6g)):
        pltpu.make_async_copy(sent.at[rest], sent.at[rest], sem).wait()
        one = pltpu.make_async_copy(sent.at[0], sent.at[0], sem)
        pl.when(home_g != gi)(one.wait)

    for here, remote in sends2:
        pl.when(jnp.logical_not(here))(remote.wait_send)
    for part in range(len(PARTS)):
        sent = piece(lines_in, part, pl.ds(0, 31))
        pltpu.make_async_copy(sent, sent, send3.at[part]).wait()
        pltpu.make_async_copy(sent, sent, send4.at[part]).wait()
    for far_copy in far_copies:
        far_copy.wait_send()


def on_device(orbitals, offsets, slot_pairs):
    plane_c, lines_c, table_c = constants()
    vmem = pl.BlockSpec(memory_space=pltpu.VMEM)
    hbm = pl.BlockSpec(memory_space=pltpu.HBM)
    dma = pltpu.SemaphoreType.DMA
    scratch = [
        pltpu.VMEM((2, PLANE, PLANE), BF16),
        pltpu.VMEM((2, 2, 256, 256), BF16),
        pltpu.VMEM((SIDE, PLANE), F32),
        pltpu.VMEM((16, 2, 16, 128), BF16),
        pltpu.VMEM((16, 2, 16, 128), BF16),
        pltpu.VMEM((4, 1, 128), F32),
        pltpu.VMEM((4, 2, 2, 16, 128), BF16),
        pltpu.VMEM((8, 1, 128), F32),
        pltpu.VMEM((8, 2, 16, 128), BF16),
        pltpu.VMEM((8, 2, 16, 128), BF16),
        pltpu.VMEM((512, 128), F32),
        pltpu.VMEM((PAIRS, 128), F32),
        pltpu.VMEM((PAIRS, 128), F32),
        pltpu.VMEM((PAIRS, 3), I32),
        pltpu.VMEM((PAIRS, PLANE), F32),
        pltpu.VMEM((PAIRS, PLANE), F32),
        pltpu.VMEM((PAIRS, PLANE), BF16),
        pltpu.VMEM((PAIRS, PLANE), BF16),
        pltpu.VMEM((PAIRS, PLANE), BF16),
        pltpu.VMEM((PAIRS, PLANE), BF16),
        pltpu.VMEM((PAIRS, PLANE), F32),
        pltpu.VMEM((32, 40, 128), F32),
        pltpu.VMEM((32, 40, 128), F32),
        pltpu.VMEM((PAIRS, PLANE), F32),
        pltpu.VMEM((PAIRS, PLANE), F32),
        pltpu.VMEM((ORB, PLANE), F32),
        pltpu.VMEM((ORB, PLANE), F32),
        pltpu.VMEM((ORB, PLANE), F32),
        pltpu.VMEM((64, 128), F32),
        pltpu.VMEM((ORB, 128), F32),
        pltpu.VMEM((ORB, 8, 128), F32),
        pltpu.VMEM((32, 8, 128), F32),
        pltpu.VMEM((ORB, 1, 128), F32),
        pltpu.VMEM((32, 1, 128), F32),
        dma((3,)),
        dma, dma,
        dma((3, 4, 2)), dma((3,)),
        dma((len(PARTS),)), dma((len(PARTS),)),
        dma((len(PARTS),)), dma((len(PARTS),)),
        dma((4,)), dma((4,)),
        dma, dma, dma, dma,
    ]
    field, gram = pl.pallas_call(
        kernel,
        out_shape=(jax.ShapeDtypeStruct((256, 128), F32), jax.ShapeDtypeStruct((1, 128), F32)),
        in_specs=[vmem, vmem, vmem, hbm, hbm, hbm],
        out_specs=(vmem, vmem),
        scratch_shapes=scratch,
        compiler_params=pltpu.CompilerParams(has_side_effects=True, collective_id=1, vmem_limit_bytes=63 * 2**20),
    )(
        orbitals,
        offsets.T,
        slot_pairs.T,
        jnp.asarray(plane_c),
        jnp.asarray(lines_c),
        jnp.asarray(table_c),
    )
    return field.reshape(1, CELLS), gram[0, :ORB].reshape(1, ORB, 1)


def solution(mesh):
    return jax.shard_map(
        on_device,
        mesh=mesh,
        in_specs=(P(("grp", "slab"), None), P(), P(("grp", "slab"), None)),
        out_specs=(P(("grp", "slab"), None), P("grp", None, "slab")),
        check_vma=False,
    )
```

```python
import math

import jax
import jax.numpy as jnp
import numpy as np
from jax import lax
from jax.experimental import pallas as pl
from jax.experimental.pallas import tpu as pltpu
from jax.sharding import PartitionSpec as P

SIDE = 32
PLANE = SIDE * SIDE
CELLS = SIDE * PLANE
CHEB = 6
GROUPS = 16
ORB = 32
PAIRS = 160
SIZES = (8, 16, 16)
PARTS = tuple((4 * sum(SIZES[:i]), n) for i, n in enumerate(SIZES))
BLOCK = 32
F32, BF16, I32 = jnp.float32, jnp.bfloat16, jnp.int32
MESH = pl.DeviceIdType.MESH

NN = (((1,), (0,)), ((), ()))
NT = (((1,), (1,)), ((), ()))
TN = (((0,), (0,)), ((), ()))


def operator_1d():
    weights = {0: -49.0 / 18.0, 1: 1.5, 2: -0.15, 3: 1.0 / 90.0}
    a = np.zeros((SIDE, SIDE))
    for i in range(SIDE):
        for j in range(SIDE):
            a[i, j] = -weights.get(abs(i - j), 0.0)
    return a


def eigen(a):
    a, n = a.copy(), a.shape[0]
    v = np.eye(n)
    for _ in range(10):
        for p in range(n - 1):
            for q in range(p + 1, n):
                if abs(a[p, q]) < 1e-18:
                    continue
                theta = (a[q, q] - a[p, p]) / (2.0 * a[p, q])
                t = (1.0 if theta >= 0 else -1.0) / (abs(theta) + math.sqrt(theta * theta + 1.0))
                c = 1.0 / math.sqrt(t * t + 1.0)
                s = t * c
                ap, aq = a[:, p].copy(), a[:, q].copy()
                a[:, p], a[:, q] = c * ap - s * aq, s * ap + c * aq
                ap, aq = a[p].copy(), a[q].copy()
                a[p], a[q] = c * ap - s * aq, s * ap + c * aq
                vp, vq = v[:, p].copy(), v[:, q].copy()
                v[:, p], v[:, q] = c * vp - s * vq, s * vp + c * vq
    return np.diag(a).copy(), v


def polynomial(lam):
    low, high = 3.0 * (math.pi / (SIDE + 1)) ** 2, 18.2
    mid, half = 0.5 * (high + low), 0.5 * (high - low)
    alpha, beta = 1.0 / mid, 0.0
    x, res, p = np.zeros_like(lam), np.ones_like(lam), np.zeros_like(lam)
    for k in range(1, CHEB + 1):
        if k > 1:
            beta = 0.5 * (half * alpha) ** 2 if k == 2 else (0.5 * half * alpha) ** 2
            alpha = 1.0 / (mid - beta / alpha)
        p = res + beta * p
        x = x + alpha * p
        res = res - alpha * lam * p
    return x


def halves(a):
    high = a.astype(BF16)
    low = (a - high.astype(np.float64)).astype(BF16)
    return np.stack([high, low])


def constants():
    lam, q = eigen(operator_1d())
    plane = halves(np.kron(q, q))
    lines = np.stack([halves(np.kron(q.T, np.eye(8))), halves(np.kron(q, np.eye(8)))])
    total = lam[:, None, None] + lam[None, :, None] + lam[None, None, :]
    table = polynomial(total).reshape(SIDE, PLANE).astype(np.float32)
    return plane, lines, table


def iota(shape, dim):
    return lax.broadcasted_iota(I32, shape, dim)


def roll(x, n, axis):
    n %= x.shape[axis]
    return pltpu.roll(x, n, axis) if n else x


def lead(x, n):
    n %= x.shape[0]
    return jnp.concatenate([x[x.shape[0] - n :], x[: x.shape[0] - n]], 0) if n else x


def bit(o, b):
    return jnp.bitwise_and(jnp.right_shift(o, b), 1) > 0


def turn_rows(x, o2, o3, sign):
    third = jnp.bitwise_and(iota(x.shape, 1), SIDE - 1)
    b2 = jnp.broadcast_to(o2, x.shape)
    b3 = jnp.broadcast_to(o3, x.shape)
    for b in range(4):
        n = 1 << b
        x = jnp.where(bit(b2, b), roll(x, sign * SIDE * n, 1), x)
        inside = third >= n if sign > 0 else third < SIDE - n
        y = jnp.where(inside, roll(x, sign * n, 1), roll(x, sign * (n - SIDE), 1))
        x = jnp.where(bit(b3, b), y, x)
    return x


def turn_box(x, o, sign):
    o1, o2, o3 = (jnp.broadcast_to(v, x.shape) for v in o)
    lane = iota(x.shape, 2)
    third = jnp.bitwise_and(lane, SIDE - 1)
    for b in range(4):
        n = 1 << b
        x = jnp.where(bit(o1, b), lead(x, sign * n), x)
        if b < 2:
            y = roll(x, sign * SIDE * n, 2)
            kept = lane >= SIDE * n if sign > 0 else lane < 128 - SIDE * n
            y = jnp.where(kept, y, roll(y, sign, 1))
        else:
            y = roll(x, sign * n // 4, 1)
        x = jnp.where(bit(o2, b), y, x)
        inside = third >= n if sign > 0 else third < SIDE - n
        y = jnp.where(inside, roll(x, sign * n, 2), roll(x, sign * (n - SIDE), 2))
        x = jnp.where(bit(o3, b), y, x)
    return x


def turn_lead(x, o1, sign):
    o = jnp.broadcast_to(o1, x.shape[1:])[None]
    for b in range(4):
        x = jnp.where(bit(o, b), lead(x, sign << b if sign > 0 else -(1 << b)), x)
    return x


def split(x):
    high = x.astype(BF16)
    return high, (x - high.astype(F32)).astype(BF16)


def dot(a, b, dims=NN):
    return lax.dot_general(a, b, dims, preferred_element_type=F32)


def three(high, low, matrix_high, matrix_low, dims=NN):
    n = high.shape[0]
    both = dot(jnp.concatenate([high, low], 0), matrix_high, dims)
    return both[:n] + both[n:] + dot(high, matrix_low, dims)


def rotated(x, y, core, t):
    m = lax.rem(t * 5, 16)
    return (
        lax.rem(x + lax.div(m, 4), 4),
        lax.rem(y + lax.rem(m, 4), 4),
        lax.rem(core + lax.div(t, 16), 2),
    )


def device(x, y, z, c):
    return x * 4 + lax.div(z, 8) * 2 + c, y * 8 + lax.rem(z, 8)


def kernel(
    box_ref, offsets_ref, slots_ref, plane_ref, lines_ref, table_ref,
    field_ref, gram_ref,
    plane, lines, table, own, mid, pair_out, boxes_out, pair_in, near_in, far_in, cells,
    ohl, ohr, offs, lm, rm, dh, dl, eh, el, modes, lines_in, lines_out, back, pots,
    field, far_field, prev_field, tiles, gp, send6, fin, gram_out, gram_fin,
    const_sem, send1, recv1, send2, recv2, send3, recv3, send4, recv4, send5, recv5,
    send6s, recv6, send6g, recv6g,
):
    gi, si = lax.axis_index("grp"), lax.axis_index("slab")
    x, zh, core = lax.div(gi, 4), lax.rem(lax.div(gi, 2), 2), lax.rem(gi, 2)
    y, zl = lax.div(si, 8), lax.rem(si, 8)
    z = zh * 8 + zl
    q = x * 4 + y
    rho = q * 2 + core
    role = z
    nxt = lax.rem(role + 1, GROUPS)

    entry = pltpu.get_barrier_semaphore()

    @pl.loop(1, 32)
    def _(t):
        peer = rotated(x, y, core, t)
        pl.semaphore_signal(entry, 1, device_id=device(peer[0], peer[1], z, peer[2]), device_id_type=MESH)

    @pl.loop(1, 16)
    def _(t):
        for c in range(2):
            pl.semaphore_signal(entry, 1, device_id=device(x, y, lax.rem(z + t, 16), c), device_id_type=MESH)

    @pl.loop(0, 32)
    def _(t):
        px, py, pc = lax.div(t, 8), lax.rem(lax.div(t, 2), 4), lax.rem(t, 2)
        other = jnp.logical_or(gi != z, jnp.logical_or(px * 4 + py != q, pc != core))

        @pl.when(other)
        def _():
            pl.semaphore_signal(entry, 1, device_id=device(px, py, gi, pc), device_id_type=MESH)

    served = jnp.where(gi == z, 31, 32)
    consts = [
        pltpu.make_async_copy(plane_ref, plane, const_sem.at[0]),
        pltpu.make_async_copy(lines_ref, lines, const_sem.at[1]),
        pltpu.make_async_copy(table_ref, table, const_sem.at[2]),
    ]
    for c in consts:
        c.start()

    row = iota((72, 512), 0)
    local = lax.rem(row, ORB)
    ident = jnp.where(row < ORB, role, nxt) * ORB + lax.rem(local, 4) * 8 + lax.div(local, 4)
    ident = jnp.where(row < 2 * ORB, ident, gi * ORB + si)
    pick = (ident == iota((72, 512), 1)).astype(BF16)
    found = dot(pick, offsets_ref[...].astype(BF16), NT)
    own_o = [found[64:65, d : d + 1].astype(I32).reshape(1, 1, 1) for d in range(3)]

    box = turn_box(box_ref[...].astype(F32).reshape(256, 128).reshape(SIDE, 8, 128), own_o, 1)
    own[:, 0] = box.reshape(16, 16, 128).astype(BF16)
    ids = slots_ref[...]
    side = iota((8, 128), 1)
    slots = jnp.full((8, 128), -1, I32)
    for k in range(6):
        at = iota((8, 128), 0) == k
        for c in range(2):
            one = jnp.broadcast_to(ids[c : c + 1, k : k + 1], (8, 128))
            slots = jnp.where(jnp.logical_and(at, side == c), one, slots)
    member = lax.rem(slots, ORB)
    spot = lax.rem(member, 8) * 4 + lax.div(member, 8)
    spot = spot + jnp.where(lax.div(slots, ORB) == gi, 0, ORB)
    spot = jnp.where(slots >= 0, spot, -1).astype(F32)
    own[:, 1] = jnp.broadcast_to(jnp.concatenate([spot, spot], 0).astype(BF16)[None], (16, 16, 128))

    pltpu.make_async_copy(own.at[q], mid.at[q], recv1).start()
    pl.semaphore_wait(entry, 61 + served)

    @pl.loop(1, 16)
    def _(t):
        px, py, _ = rotated(x, y, core, t)
        pltpu.make_async_remote_copy(
            own.at[px * 4 + py], mid.at[q], send1, recv1, device(px, py, z, core), MESH
        ).start()

    pltpu.make_async_copy(mid, mid, recv1).wait()

    heap = mid[:, 0].astype(F32).reshape(4, 4, 2, 8, 128)
    lists = mid[:, 1].astype(F32)[:, :8].reshape(4, 4, 8, 128)
    row8, lane8 = iota((8, 128), 0), iota((8, 128), 1)
    for g in range(4):
        merged = jnp.where(lane8 < 2, lists[g, 0], 0.0)
        for j in range(1, 4):
            merged = merged + jnp.where(lax.div(lane8, 2) == j, roll(lists[g, j], 2 * j, 1), 0.0)
        spread = merged
        for t in range(1, 6):
            spread = spread + roll(merged, 8 * t, 1)
        spread = jnp.where(lax.div(lane8, 8) == row8, spread, 0.0)
        pair_out[g] = jnp.sum(spread, axis=0, keepdims=True)
        for c in range(2):
            part = heap[g, :, c].reshape(2, 16, 128).astype(BF16)
            boxes_out[g, c] = part
    sends2 = []
    for kind in range(3):
        for k in range(4):
            g = lax.rem(k + zl, 4)
            for c in range(2):
                target = lax.rem(g * 4 + zh * 2 + core + GROUPS - (1 if kind == 2 else 0), GROUPS)
                here = jnp.logical_and(target == z, core == c)
                out = pair_out.at[g] if kind == 0 else boxes_out.at[g, c]
                into = (pair_in, near_in, far_in)[kind].at[zl]
                remote = pltpu.make_async_remote_copy(
                    out, into, send2.at[kind, k, c], recv2.at[kind], device(x, y, target, c), MESH
                )
                local_copy = pltpu.make_async_copy(out, into, recv2.at[kind])
                pl.when(here)(local_copy.start)
                pl.when(jnp.logical_not(here))(remote.start)
                sends2.append((here, remote))
    pltpu.make_async_copy(own.at[pl.ds(0, 15)], own.at[pl.ds(0, 15)], send1).wait()
    pltpu.make_async_copy(pair_in, pair_in, recv2.at[0]).wait()

    lists = pair_in[...].reshape(8, 128)
    spots = [(8 * t + 2 * j) for t in range(6) for j in range(4)]
    left = jnp.concatenate([lists[:, a : a + 1] for a in spots], 0)
    right = jnp.concatenate([lists[:, a + 1 : a + 2] for a in spots], 0)
    live = left >= 0
    live_f = jnp.where(live, 1.0, 0.0)
    before = (iota((192, 192), 1) < iota((192, 192), 0)).astype(BF16)
    rank = dot(before, jnp.broadcast_to(live_f, (192, 128)).astype(BF16))[:, 0:1]
    rank = jnp.where(live, rank, -1.0)
    chosen = (jnp.broadcast_to(rank, (192, 256)) == iota((192, 256), 1).astype(F32)).astype(BF16)
    orbital = iota((192, 128), 1).astype(F32)
    pick_l = (jnp.broadcast_to(left, (192, 128)) == orbital).astype(BF16)
    pick_r = (jnp.broadcast_to(right, (192, 128)) == orbital).astype(BF16)
    one_l = dot(chosen, pick_l, TN)[:PAIRS]
    one_r = dot(chosen, pick_r, TN)[:PAIRS]
    ohl[...] = one_l
    ohr[...] = one_r
    o3 = jnp.concatenate([found[:64], jnp.zeros((64, found.shape[1]), F32)], 0)
    offs[...] = jnp.broadcast_to(dot(one_l.astype(BF16), o3.astype(BF16))[:, :3], (PAIRS, 3)).astype(I32)

    lane = iota((64, PLANE), 1)
    o = [jnp.broadcast_to(found[:64, d : d + 1], (64, PLANE)) for d in range(3)]
    code = jnp.where(rho.astype(F32) < o[0], 1.0, 0.0)
    code = code + jnp.where(lax.div(lane, SIDE).astype(F32) < o[1], 2.0, 0.0)
    code = code + jnp.where(jnp.bitwise_and(lane, SIDE - 1).astype(F32) < o[2], 4.0, 0.0)
    pltpu.make_async_copy(near_in, near_in, recv2.at[1]).wait()
    pltpu.make_async_copy(far_in, far_in, recv2.at[2]).wait()
    cells[0:256] = near_in[...].astype(F32).reshape(256, 128)
    cells[256:512] = far_in[...].astype(F32).reshape(256, 128)
    orbs = jnp.concatenate([cells[pl.ds(r, 64, stride=8), :] for r in range(8)], 1)
    both = jnp.concatenate([orbs, code], 1).astype(BF16)
    both = jnp.concatenate([both, jnp.zeros((64, 2 * PLANE), BF16)], 0)

    for b in range(PAIRS // BLOCK):
        rows = slice(b * BLOCK, (b + 1) * BLOCK)
        lv = dot(ohl[rows].astype(BF16), both)
        rv = dot(ohr[rows].astype(BF16), both)
        same = lv[:, PLANE:] == rv[:, PLANE:]
        lmv = jnp.where(same, lv[:, :PLANE], 0.0)
        rmv = jnp.where(same, rv[:, :PLANE], 0.0)
        lm[rows] = lmv
        rm[rows] = rmv
        dens = turn_rows(lmv * rmv, offs[rows, 1:2], offs[rows, 2:3], -1)
        dh[rows], dl[rows] = split(dens)

    for c in consts:
        c.wait()

    def part_of(ref, r, part):
        base, size = PARTS[part]
        return ref.at[
            pl.ds(pl.multiple_of(base + lax.div(r, 8) * size, 8), size),
            pl.ds(pl.multiple_of(lax.rem(r, 8) * 128, 128), 128),
        ]

    def piece(ref, part, at=slice(None)):
        base, size = PARTS[part]
        return ref.at[at, base // 4 : base // 4 + size]

    for part, (base, size) in enumerate(PARTS):
        rows = slice(base, base + 4 * size)
        landing = piece(lines_in, part, rho)
        for dy in (2, 1, 3, 0):
            py = lax.rem(y + dy, 4)
            cols = pl.ds(pl.multiple_of(py * 256, 256), 256)
            wh, wl = plane[0, :, cols], plane[1, :, cols]
            modes[rows, cols] = three(dh[rows], dl[rows], wh, wl)
            for dx in (2, 1, 3, 0):
                for dc in (1, 0):
                    px, pc = lax.rem(x + dx, 4), lax.rem(core + dc, 2)
                    out = part_of(modes, px * 8 + py * 2 + pc, part)
                    if (dx, dy, dc) == (0, 0, 0):
                        pltpu.make_async_copy(out, landing, recv3.at[part]).start()
                    else:
                        pltpu.make_async_remote_copy(
                            out, landing, send3.at[part], recv3.at[part], device(px, py, z, pc), MESH
                        ).start()

    u, v = lax.div(rho, 8), lax.rem(rho, 8)
    scale = table[:, pl.ds(pl.multiple_of(v * 128, 128), 128)]
    scale = jnp.broadcast_to(scale[:, None, :], (SIDE, 8, 128)).reshape(256, 128)
    for part, (base, size) in enumerate(PARTS):
        pltpu.make_async_copy(piece(lines_in, part), piece(lines_in, part), recv3.at[part]).wait()
        for j in range(size // 8):
            rows = slice(base // 4 + 8 * j, base // 4 + 8 * j + 8)
            o1 = offs[pl.ds(pl.multiple_of(base + u * size + 8 * j, 8), 8), 0:1]
            s = turn_lead(lines_in[:, rows, :], o1, -1).reshape(256, 128)
            for way in range(2):
                sh, sl = split(s)
                both = dot(lines[way].reshape(512, 256), sh)
                s = both[:256] + both[256:] + dot(lines[way, 0], sl)
                if way == 0:
                    s = s * scale
            lines_out[:, rows, :] = turn_lead(s.reshape(SIDE, 8, 128), o1, 1)

        landing = part_of(back, rho, part)
        pltpu.make_async_copy(piece(lines_out, part, rho), landing, recv4.at[part]).start()

        @pl.loop(1, 32)
        def _(t):
            px, py, pc = rotated(x, y, core, t)
            r = px * 8 + py * 2 + pc
            pltpu.make_async_remote_copy(
                piece(lines_out, part, r), landing, send4.at[part], recv4.at[part], device(px, py, z, pc), MESH
            ).start()

    for part, (base, size) in enumerate(PARTS):
        rows = slice(base, base + 4 * size)
        arrived = back.at[pl.ds(base, 4 * size)]
        pltpu.make_async_copy(arrived, arrived, recv4.at[part]).wait()
        dh[rows], dl[rows] = split(back[rows])
        for n in range(4):
            cols = slice(n * 256, (n + 1) * 256)
            wh, wl = plane[0, cols, :], plane[1, cols, :]
            pots[rows, cols] = three(dh[rows], dl[rows], wh, wl, NT)
        for b in range(4 * size // BLOCK):
            rows = slice(base + b * BLOCK, base + (b + 1) * BLOCK)
            pot = turn_rows(pots[rows], offs[rows, 1:2], offs[rows, 2:3], 1)
            pots[rows] = pot
            dh[rows], dl[rows] = split(pot * lm[rows])
        rows = slice(base, base + 4 * size)
        pick_f = ohr[rows, ORB : 2 * ORB].astype(BF16)
        term = dot(pick_f, dh[rows], TN) + dot(pick_f, dl[rows], TN)
        far_field[...] = far_field[...] + term if part else term
    far_copies = []
    for t in range(4):
        k = lax.rem(lax.div(lax.rem(zl + 1, 8), 2) + t, 4)
        rows = pl.ds(pl.multiple_of(8 * k, 8), 8)
        far_copies.append(
            pltpu.make_async_remote_copy(
                far_field.at[rows], prev_field.at[rows], send5.at[t], recv5.at[k], device(x, y, nxt, core), MESH
            )
        )
        far_copies[-1].start()
    pick_f = ohr[:, 0:ORB].astype(BF16)
    total = dot(pick_f, dh[...], TN) + dot(pick_f, dl[...], TN)
    for b in range(PAIRS // BLOCK):
        rows = slice(b * BLOCK, (b + 1) * BLOCK)
        eh[rows], el[rows] = split(pots[rows] * rm[rows])
    pick_f = ohl[:, 0:ORB].astype(BF16)
    field[...] = total + dot(pick_f, eh[...], TN) + dot(pick_f, el[...], TN)
    framed = jnp.where(code[:ORB] == code[0:1], orbs[:ORB], 0.0)
    perm_row = iota((128, ORB), 0)
    perm = (lax.rem(perm_row, 8) * 4 + lax.div(perm_row, 8) == iota((128, ORB), 1)) & (perm_row < ORB)
    framed = dot(perm.astype(BF16), framed.astype(BF16)).astype(BF16)
    home_x, home_zh, home_c = lax.div(role, 4), lax.rem(lax.div(role, 2), 2), lax.rem(role, 2)
    home_g = home_x * 4 + home_zh * 2 + home_c

    def send_home(k, j, out, into, send, recv):
        here = jnp.logical_and(home_g == gi, j * 8 + k == si)
        remote = pltpu.make_async_remote_copy(out, into, send, recv, (home_g, j * 8 + k), MESH)
        pl.when(here)(pltpu.make_async_copy(out, into, recv).start)
        pl.when(jnp.logical_not(here))(remote.start)

    for t in range(4):
        pair = lax.rem(lax.div(zl, 2) + t, 4)
        rows = pl.ds(pl.multiple_of(8 * pair, 8), 8)
        arrived = prev_field.at[rows]
        pltpu.make_async_copy(arrived, arrived, recv5.at[pair]).wait()
        summed = field[rows] + prev_field[rows]
        field[rows] = summed
        for r in range(8):
            tiles[pl.ds(r, 8, stride=8), :] = summed[:, r * 128 : (r + 1) * 128]
        send6[pl.ds(pl.multiple_of(8 * pair, 8), 8)] = tiles[...].reshape(8, 8, 128)

        @pl.loop(0, 8)
        def _(i):
            k, j = 2 * pair + lax.rem(i, 2), lax.rem(y + lax.div(i, 2), 4)
            send_home(k, j, send6.at[4 * k + j], fin.at[rho], send6s, recv6)

    framed_field = jnp.where(code[:ORB] == code[0:1], field[...], 0.0).astype(BF16)
    gp[...] = dot(framed_field, framed, NT)
    for k in range(ORB):
        gram_out[k] = gp[k : k + 1]

    @pl.loop(0, ORB)
    def _(i):
        k, j = lax.rem(zl + lax.rem(i, 8), 8), lax.rem(y + lax.div(i, 8), 4)
        send_home(k, j, gram_out.at[4 * k + j], gram_fin.at[rho], send6g, recv6g)

    pltpu.make_async_copy(fin, fin, recv6).wait()
    field_ref[...] = turn_box(fin[...], own_o, -1).reshape(256, 128)
    pltpu.make_async_copy(gram_fin, gram_fin, recv6g).wait()
    gram_ref[...] = jnp.sum(gram_fin[...], axis=0) * (1.0 / math.sqrt(CELLS))

    rest = pl.ds(0, 31)
    for sent, sem in ((fin, send6s), (gram_fin, send6g)):
        pltpu.make_async_copy(sent.at[rest], sent.at[rest], sem).wait()
        one = pltpu.make_async_copy(sent.at[0], sent.at[0], sem)
        pl.when(home_g != gi)(one.wait)

    for here, remote in sends2:
        pl.when(jnp.logical_not(here))(remote.wait_send)
    for part in range(len(PARTS)):
        sent = piece(lines_in, part, pl.ds(0, 31))
        pltpu.make_async_copy(sent, sent, send3.at[part]).wait()
        pltpu.make_async_copy(sent, sent, send4.at[part]).wait()
    for far_copy in far_copies:
        far_copy.wait_send()


def on_device(orbitals, offsets, slot_pairs):
    plane_c, lines_c, table_c = constants()
    vmem = pl.BlockSpec(memory_space=pltpu.VMEM)
    hbm = pl.BlockSpec(memory_space=pltpu.HBM)
    dma = pltpu.SemaphoreType.DMA
    scratch = [
        pltpu.VMEM((2, PLANE, PLANE), BF16),
        pltpu.VMEM((2, 2, 256, 256), BF16),
        pltpu.VMEM((SIDE, PLANE), F32),
        pltpu.VMEM((16, 2, 16, 128), BF16),
        pltpu.VMEM((16, 2, 16, 128), BF16),
        pltpu.VMEM((4, 1, 128), F32),
        pltpu.VMEM((4, 2, 2, 16, 128), BF16),
        pltpu.VMEM((8, 1, 128), F32),
        pltpu.VMEM((8, 2, 16, 128), BF16),
        pltpu.VMEM((8, 2, 16, 128), BF16),
        pltpu.VMEM((512, 128), F32),
        pltpu.VMEM((PAIRS, 128), F32),
        pltpu.VMEM((PAIRS, 128), F32),
        pltpu.VMEM((PAIRS, 3), I32),
        pltpu.VMEM((PAIRS, PLANE), F32),
        pltpu.VMEM((PAIRS, PLANE), F32),
        pltpu.VMEM((PAIRS, PLANE), BF16),
        pltpu.VMEM((PAIRS, PLANE), BF16),
        pltpu.VMEM((PAIRS, PLANE), BF16),
        pltpu.VMEM((PAIRS, PLANE), BF16),
        pltpu.VMEM((PAIRS, PLANE), F32),
        pltpu.VMEM((32, 40, 128), F32),
        pltpu.VMEM((32, 40, 128), F32),
        pltpu.VMEM((PAIRS, PLANE), F32),
        pltpu.VMEM((PAIRS, PLANE), F32),
        pltpu.VMEM((ORB, PLANE), F32),
        pltpu.VMEM((ORB, PLANE), F32),
        pltpu.VMEM((ORB, PLANE), F32),
        pltpu.VMEM((64, 128), F32),
        pltpu.VMEM((ORB, 128), F32),
        pltpu.VMEM((ORB, 8, 128), F32),
        pltpu.VMEM((32, 8, 128), F32),
        pltpu.VMEM((ORB, 1, 128), F32),
        pltpu.VMEM((32, 1, 128), F32),
        dma((3,)),
        dma, dma,
        dma((3, 4, 2)), dma((3,)),
        dma((len(PARTS),)), dma((len(PARTS),)),
        dma((len(PARTS),)), dma((len(PARTS),)),
        dma((4,)), dma((4,)),
        dma, dma, dma, dma,
    ]
    field, gram = pl.pallas_call(
        kernel,
        out_shape=(jax.ShapeDtypeStruct((256, 128), F32), jax.ShapeDtypeStruct((1, 128), F32)),
        in_specs=[vmem, vmem, vmem, hbm, hbm, hbm],
        out_specs=(vmem, vmem),
        scratch_shapes=scratch,
        compiler_params=pltpu.CompilerParams(has_side_effects=True, collective_id=1, vmem_limit_bytes=63 * 2**20),
    )(
        orbitals,
        offsets.T,
        slot_pairs.T,
        jnp.asarray(plane_c),
        jnp.asarray(lines_c),
        jnp.asarray(table_c),
    )
    return field.reshape(1, CELLS), gram[0, :ORB].reshape(1, ORB, 1)


def solution(mesh):
    return jax.shard_map(
        on_device,
        mesh=mesh,
        in_specs=(P(("grp", "slab"), None), P(), P(("grp", "slab"), None)),
        out_specs=(P(("grp", "slab"), None), P("grp", None, "slab")),
        check_vma=False,
    )
```
